32 devices in a mesh: dp: 4 (over y, x), expert: 8 (over z, core).
Axes of the slice: x: 2, y: 2, z: 4, core: 2. Of those that a mesh axis runs over, the one named last changes fastest.
Arguments:
- tokens: bfloat16 [512, 3584], P(('dp', 'expert')), may hold values from -6 to 6
- out_grad: bfloat16 [512, 3584], P(('dp', 'expert')), may hold values from -6 to 6
- route_ids: int32 [512, 8], P(('dp', 'expert')), may hold values from 0 to 15, all different within a row; in each aligned block of 16 rows (0 to 15, 16 to 31, ...) at most 16 rows name the same one
- route_probs: float32 [512, 8], P(('dp', 'expert')), may hold values from 0.02 to 0.5
- w_gate: bfloat16 [16, 3584, 1024], P('expert', None, 'dp'), may hold values from -0.09375 to 0.09375
- w_up: bfloat16 [16, 3584, 1024], P('expert', None, 'dp'), may hold values from -0.09375 to 0.09375
- w_down: bfloat16 [16, 1024, 3584], P('expert', 'dp'), may hold values from -0.1875 to 0.1875
Outputs:
- in_grad: bfloat16 [512, 3584], P(('dp', 'expert'))
The draws below stay inside these ranges and needn't reach their ends.
Inputs may be any that keep to these rules, and one draw needn't show every extreme that they name: `route_ids`: the 8 ids of a token differ. Among the tokens of one device (aligned blocks of 16 rows) no expert is named more than 16 times, and in every draw some expert is named exactly 16 times there.
All inputs are finite; a program needn't handle non-finite values.
Results may differ from the reference program's by a relative error of at most 0.015.
Values may be sent and summed in bfloat16 or wider, within the bound.
A program may use at most 128 MiB of HBM per device.

```python
import math
import jax
import jax.numpy as jnp
import numpy as np
from jax import lax

D = 3584
H = 1024
TOPK = 8
TOK_DEV = 16
EXPERTS = 16
CAP = 16
TOKENS = 512
N_DP = 4


def block_scale(stream_key, dims, cuts, smallest, top_value):
    loudness, own = 1.0, jax.random.fold_in(stream_key, 6)
    for axis_at, blocks in cuts:
        heights = jnp.exp(jax.random.uniform(jax.random.fold_in(own, axis_at), (blocks,), jnp.float32, smallest / len(cuts), top_value / len(cuts)))
        loudness = loudness * jnp.repeat(heights, dims[axis_at] // blocks).reshape([-1 if axis == axis_at else 1 for axis in range(len(dims))])
    return loudness


def shared_out(key, own, number, rows, amount, top, bound, slope):
    order = jax.random.permutation(key, amount)
    packed, ordinary = portions_of(amount, rows * top, bound, slope, True), portions_of(amount, rows * top, bound, slope, False)
    places = jnp.arange(amount)

    def named(sizes, rotation):
        used = int((sizes > 0).sum())
        fixed = max(1, used // 4)
        shifted = fixed + (places - fixed + rotation * (used - fixed)) % max(1, amount - fixed)
        return jnp.zeros((amount,), jnp.int32).at[order[jnp.where(places < fixed, places, shifted)]].set(jnp.asarray(sizes, jnp.int32))

    sizes = jnp.where(number % 4 == 0, named(packed, number // 4), named(ordinary, number - number // 4 - 1))
    mixed = jax.random.permutation(jax.random.fold_in(own, 3), amount)
    giver, sink = mixed[0:amount // 2 * 2:2], mixed[1:amount // 2 * 2:2]
    room = jnp.minimum(sizes[giver] - 1, bound - sizes[sink]) // 2
    room = jnp.where((giver == order[0]) | (sink == order[0]) | (sizes[sink] == 0), 0, jnp.maximum(room, 0))
    shifted = jax.random.randint(jax.random.fold_in(own, 4), (amount // 2,), 0, 1 << 20) % (room + 1)
    sizes = sizes.at[giver].add(-shifted).at[sink].add(shifted)
    members = jnp.searchsorted(jnp.cumsum(sizes), jnp.arange(rows * top), side="right").astype(jnp.int32)
    grid = members.reshape(top, rows).T
    grid = grid[jax.random.permutation(jax.random.fold_in(own, 1), rows)]
    rotation = jax.random.randint(jax.random.fold_in(own, 2), (rows, 1), 0, top)
    return jnp.take_along_axis(grid, (jnp.arange(top)[None, :] + rotation) % top, axis=1)


def portions_of(number_of, total, limit, slope, full):
    weights = [(1 << 20) // math.isqrt(rank ** slope) + 1 for rank in range(1, number_of + 1)]
    largest = limit if full else min(limit, max(-(-total // number_of), total * weights[0] // sum(weights)))
    least = 1 if total - largest >= number_of - 1 else 0
    holding, surplus = [largest] + [least] * (number_of - 1), total - largest - least * (number_of - 1)
    while surplus > 0:
        movable = [i for i in range(1, number_of) if holding[i] < largest] or [i for i in range(1, number_of) if holding[i] < limit]
        mass, left = sum([weights[i] for i in movable]), surplus
        for i in movable:
            more = min(limit - holding[i], max(1, left * weights[i] // mass), surplus)
            holding[i] = holding[i] + more
            surplus = surplus - more
    return np.array(holding)


def gaussian(key, dims, scale, most, cuts=(), held_as=jnp.bfloat16):
    values = scale * jax.random.normal(key, dims, jnp.float32)
    if cuts:
        values = values * block_scale(key, dims, cuts, -0.22, 0.18)
    return jnp.clip(values, -most, most).astype(held_as)


def setup_inputs(seed: int = 0) -> dict:
    keys = jax.random.split(jax.random.key(seed), 8)
    tokens = gaussian(keys[0], (TOKENS, D), 1.0, 6.0, ((0, 32),))
    out_grad = gaussian(keys[1], (TOKENS, D), 1.0, 6.0, ((0, 32),))
    route_ids_keys = jax.random.split(jax.random.fold_in(keys[2], 1), TOKENS // TOK_DEV)
    route_ids_turns = jax.random.permutation(jax.random.fold_in(keys[2], 3), TOKENS // TOK_DEV)
    route_ids = jax.vmap(lambda own, number: shared_out(jax.random.fold_in(keys[2], 2), own, number, TOK_DEV, EXPERTS, TOPK, CAP, 2))(route_ids_keys, route_ids_turns).reshape((TOKENS, TOPK))
    route_probs = jnp.clip(jnp.exp(math.log(0.5) - 3.218876 * jax.random.uniform(keys[3], (TOKENS, TOPK), jnp.float32) ** block_scale(keys[3], (TOKENS, TOPK), ((0, 32),), -0.2, 0.2)), 0.02, 0.5)
    w_gate = gaussian(keys[4], (EXPERTS, D, H), D ** -0.5, 0.09375, ((0, 8), (2, 4)))
    w_up = gaussian(keys[5], (EXPERTS, D, H), D ** -0.5, 0.09375, ((0, 8), (2, 4)))
    w_down = gaussian(keys[6], (EXPERTS, H, D), H ** -0.5, 0.1875, ((0, 8), (1, 4)))
    return dict(tokens=tokens, out_grad=out_grad, route_ids=route_ids, route_probs=route_probs, w_gate=w_gate, w_up=w_up, w_down=w_down)


def reference(tokens, out_grad, route_ids, route_probs, w_gate, w_up, w_down):
    experts = w_gate.shape[0]
    tok_total = tokens.shape[0]
    width = tokens.shape[1]
    blocks = tok_total // TOK_DEV
    per_block = TOK_DEV * TOPK
    block_ids = route_ids.reshape(blocks, per_block)
    onehot = (block_ids[:, :, None] == jnp.arange(experts, dtype=jnp.int32)[None, None, :]).astype(jnp.int32)
    slot_rank = jnp.sum((jnp.cumsum(onehot, axis=1) - onehot) * onehot, axis=2)
    block_index = (jnp.arange(blocks * per_block, dtype=jnp.int32) // per_block).reshape(blocks, per_block)
    table_row = (block_index * CAP + slot_rank).reshape(-1)
    flat_expert = route_ids.reshape(-1)
    token_index = jnp.arange(tok_total * TOPK, dtype=jnp.int32) // TOPK
    table_width = blocks * CAP
    table = jnp.full((experts, table_width), tok_total, dtype=jnp.int32).at[flat_expert, table_row].set(token_index)
    weights = jnp.zeros((experts, table_width), jnp.float32).at[flat_expert, table_row].set(route_probs.reshape(-1))
    zero_row = jnp.zeros((1, width), tokens.dtype)
    padded_tokens = jnp.concatenate([tokens, zero_row], axis=0)
    padded_grads = jnp.concatenate([out_grad, zero_row], axis=0)
    quarter = w_gate.shape[2] // N_DP

    def one_expert(carry, expert):
        rows = table[expert]
        x_rows = padded_tokens[rows]
        g_rows = (padded_grads[rows].astype(jnp.float32) * weights[expert][:, None]).astype(jnp.bfloat16)
        gate_w = w_gate[expert]
        up_w = w_up[expert]
        down_w = w_down[expert]
        gate_pre = jnp.dot(x_rows, gate_w, preferred_element_type=jnp.float32)
        up_pre = jnp.dot(x_rows, up_w, preferred_element_type=jnp.float32)
        hidden_grad = jnp.dot(g_rows, down_w.T, preferred_element_type=jnp.float32)
        sigmoid_a = jax.nn.sigmoid(gate_pre)
        gate_grad = (hidden_grad * up_pre * sigmoid_a * (1.0 + gate_pre * (1.0 - sigmoid_a))).astype(jnp.bfloat16)
        up_grad = (hidden_grad * gate_pre * sigmoid_a).astype(jnp.bfloat16)
        total = jnp.zeros((rows.shape[0], width), jnp.float32)
        for block in range(N_DP):
            low = block * quarter
            high = low + quarter
            partial_value = jnp.dot(gate_grad[:, low:high], gate_w[:, low:high].T, preferred_element_type=jnp.float32)
            partial_value = partial_value + jnp.dot(up_grad[:, low:high], up_w[:, low:high].T, preferred_element_type=jnp.float32)
            total = total + partial_value.astype(jnp.bfloat16).astype(jnp.float32)
        return carry.at[rows].add(total), None

    start = jnp.zeros((tok_total + 1, width), jnp.float32)
    final, unused = lax.scan(one_expert, start, jnp.arange(experts, dtype=jnp.int32))
    return final[:tok_total].astype(jnp.bfloat16)
```

```python
import jax
import jax.numpy as jnp
from jax import lax
from jax.experimental import pallas as pl
from jax.experimental.pallas import tpu as pltpu
from jax.sharding import PartitionSpec as P

TOPK = 8
LANES = 128
MESH = pl.DeviceIdType.MESH
BF16 = jnp.bfloat16
F32 = jnp.float32
COPIES = 64
NT = (((1,), (1,)), ((), ()))


def fused_kernel(
    tokens_ref, grads_ref, ids_ref, probs_ref, w_gate_ref, w_up_ref, w_down_ref, out_ref,
    rows_buf, w_cat, w_dn, acc_in, acc_hid, hid_grads, part, core_got, pair_sum,
    x_got, y_got, send2, got2, column, z_got, send_sems, recv_sems, weight_sems,
):
    dp, ex = lax.axis_index("dp"), lax.axis_index("expert")
    y, x = dp // 2, dp % 2
    z, c = ex // 2, ex % 2
    oy, ox, oc = 1 - y, 1 - x, 1 - c
    to_x, to_y, to_core = (y * 2 + ox, ex), (oy * 2 + x, ex), (dp, z * 2 + oc)
    to_z = {k: (dp, ((z + k) % 4) * 2 + c) for k in (1, 2, 3)}
    width = tokens_ref.shape[1]
    half_w = width // 2
    local, _, hid = w_gate_ref.shape
    started = []

    def send(src, dst, device):
        at = len(started)
        copy = pltpu.make_async_remote_copy(
            src_ref=src, dst_ref=dst, send_sem=send_sems.at[at], recv_sem=recv_sems.at[at],
            device_id=device, device_id_type=MESH,
        )
        copy.start()
        started.append(copy)
        return copy

    barrier = pltpu.get_barrier_semaphore()
    for device in (to_x, to_y, to_core, to_z[1], to_z[2], to_z[3]):
        pl.semaphore_signal(barrier, inc=1, device_id=device, device_id_type=MESH)

    weight_copies = []
    for e in range(local):
        for n, ref in enumerate((w_gate_ref, w_up_ref)):
            weight_copies.append(
                pltpu.make_async_copy(
                    ref.at[e], w_cat.at[:, pl.ds((2 * e + n) * hid, hid)], weight_sems.at[2 * e + n]
                )
            )
    weight_copies.append(pltpu.make_async_copy(w_down_ref, w_dn, weight_sems.at[2 * local]))
    for copy in weight_copies:
        copy.start()

    lane = lax.broadcasted_iota(jnp.int32, (tokens_ref.shape[0], LANES), 1)
    weights = jnp.zeros(lane.shape, F32)
    for k in range(TOPK):
        weights = weights + jnp.where(ids_ref[:, k : k + 1] == lane, probs_ref[:, k : k + 1], 0.0)
    high = weights.astype(BF16)
    rows_buf[y, x, z, c, 0, :, :width] = tokens_ref[...]
    rows_buf[y, x, z, c, 1, :, :width] = grads_ref[...]
    rows_buf[y, x, z, c, 0, :, width:] = high
    rows_buf[y, x, z, c, 1, :, width:] = (weights - high.astype(F32)).astype(BF16)

    pl.semaphore_wait(barrier, 6)

    def block(by, bx, bz):
        return rows_buf.at[by, bx, bz, c]

    own = block(y, x, z)
    x_in, y_in, core_col, core_x, core_y, diag_in, core_diag = [], [], [], [], [], [], []
    x_in.append(send(own, own, to_x))
    y_in.append(send(own, own, to_y))
    z_in = {k: send(own, own, to_z[k]) for k in (1, 3, 2)}
    core_col.append(send(own, own, to_core))
    order = [z]
    for k in (1, 3, 2):
        z_in[k].wait_recv()
        s = (z + 4 - k) % 4
        order.append(s)
        got = block(y, x, s)
        x_in.append(send(got, got, to_x))
        y_in.append(send(got, got, to_y))
        core_col.append(send(got, got, to_core))
    for i, s in enumerate(order):
        x_in[i].wait_recv()
        got = block(y, ox, s)
        low = got.at[0]
        diag_in.append(send(low, low, to_y))
        core_x.append(send(got, got, to_core))
        y_in[i].wait_recv()
        got = block(oy, x, s)
        low = got.at[1]
        diag_in.append(send(low, low, to_x))
        core_y.append(send(got, got, to_core))
    for copy in weight_copies:
        copy.wait()
    for copy in core_col + core_x:
        copy.wait_recv()

    rows = 16 * tokens_ref.shape[0]
    k_tile = 512
    o_tile = 256

    def hidden(by):
        acc_in[...] = jnp.zeros_like(acc_in)
        acc_hid[...] = jnp.zeros_like(acc_hid)

        @pl.loop(0, width // k_tile)
        def _(k):
            cols = pl.ds(pl.multiple_of(k * k_tile, k_tile), k_tile)
            x_rows = rows_buf[by, :, :, :, 0, :, cols].reshape(rows, k_tile)
            g_rows = rows_buf[by, :, :, :, 1, :, cols].reshape(rows, k_tile)
            acc_in[...] += jnp.dot(x_rows, w_cat[cols, :], preferred_element_type=F32)
            down = w_dn[:, :, cols].reshape(local * hid, k_tile)
            acc_hid[...] += lax.dot_general(g_rows, down, NT, preferred_element_type=F32)

        tail = pl.ds(width, LANES)
        wts = rows_buf[by, :, :, :, 0, :, tail].reshape(rows, LANES).astype(F32)
        wts = wts + rows_buf[by, :, :, :, 1, :, tail].reshape(rows, LANES).astype(F32)
        which = lax.broadcasted_iota(jnp.int32, (rows, LANES), 1)
        for e in range(local):
            scale = jnp.sum(jnp.where(which == ex * local + e, wts, 0.0), axis=1, keepdims=True)
            gate = acc_in[:, 2 * e * hid : (2 * e + 1) * hid]
            up = acc_in[:, (2 * e + 1) * hid : (2 * e + 2) * hid]
            grad = acc_hid[:, e * hid : (e + 1) * hid] * scale
            s = jax.nn.sigmoid(gate)
            hid_grads[:, 2 * e * hid : (2 * e + 1) * hid] = (
                grad * up * s * (1.0 + gate * (1.0 - s))
            ).astype(BF16)
            hid_grads[:, (2 * e + 1) * hid : (2 * e + 2) * hid] = (grad * gate * s).astype(BF16)

    def project(h, half):
        @pl.loop(0, half_w // o_tile)
        def _(j):
            local_cols = pl.ds(pl.multiple_of(j * o_tile, o_tile), o_tile)
            w_rows = pl.ds(pl.multiple_of(half * half_w + j * o_tile, o_tile), o_tile)
            value = lax.dot_general(hid_grads[...], w_cat[w_rows, :], NT, preferred_element_type=F32)
            value = value.astype(BF16).reshape(2, 4, 2, rows // 16, o_tile)
            part[h, half, 0, :, :, :, local_cols] = value[:, :, 0]
            part[h, half, 1, :, :, :, local_cols] = value[:, :, 1]

        return send(part.at[h, half, oc], core_got.at[h, half], to_core)

    def add_cores(h, half, copy):
        copy.wait_recv()

        @pl.loop(0, 4)
        def _(b):
            pair_sum[h, half, :, b] = (
                part[h, half, c, :, b].astype(F32) + core_got[h, half, :, b].astype(F32)
            ).astype(BF16)

    hidden(y)
    core0 = [project(0, 0), project(0, 1)]
    for i, s in enumerate(order):
        for n in range(2):
            diag_in[2 * i + n].wait_recv()
            got = block(oy, ox, s).at[n]
            core_diag.append(send(got, got, to_core))
    add_cores(0, 0, core0[0])
    rx0 = send(pair_sum.at[0, 0, ox], x_got.at[0], to_x)
    add_cores(0, 1, core0[1])
    for copy in core_y + core_diag:
        copy.wait_recv()
    hidden(oy)
    core1b = project(1, 1)
    core1a = project(1, 0)
    add_cores(1, 1, core1b)
    ry = send(pair_sum.at[1, 1], y_got, to_y)
    add_cores(1, 0, core1a)
    rx1 = send(pair_sum.at[1, 0, ox], x_got.at[1], to_x)

    rx1.wait_recv()

    @pl.loop(0, 4)
    def _(b):
        send2[0, b] = (pair_sum[1, 0, x, b].astype(F32) + x_got[1, b].astype(F32)).astype(BF16)

    ry2 = send(send2.at[0], got2.at[0], to_y)
    ry.wait_recv()

    @pl.loop(0, 4)
    def _(b):
        send2[1, b] = (pair_sum[0, 1, ox, b].astype(F32) + y_got[ox, b].astype(F32)).astype(BF16)

    rx2 = send(send2.at[1], got2.at[1], to_x)
    rx0.wait_recv()
    ry2.wait_recv()

    @pl.loop(0, 4)
    def _(b):
        column[0, b] = (
            pair_sum[0, 0, x, b].astype(F32) + x_got[0, b].astype(F32) + got2[0, b].astype(F32)
        ).astype(BF16)

    z_out = [[], []]
    for k in (2, 1, 3):
        z_out[0].append(send(column.at[0, (z + k) % 4], z_got.at[0, k - 1], to_z[k]))
    rx2.wait_recv()

    @pl.loop(0, 4)
    def _(b):
        column[1, b] = (
            pair_sum[0, 1, x, b].astype(F32) + y_got[x, b].astype(F32) + got2[1, b].astype(F32)
        ).astype(BF16)

    for k in (2, 1, 3):
        z_out[1].append(send(column.at[1, (z + k) % 4], z_got.at[1, k - 1], to_z[k]))
    for half in range(2):
        for copy in z_out[half]:
            copy.wait_recv()
        total = column[half, z].astype(F32)
        for k in range(3):
            total = total + z_got[half, k].astype(F32)
        out_ref[:, half * half_w : (half + 1) * half_w] = total.astype(BF16)
    for copy in started:
        copy.wait_send()


def fused(tokens, out_grad, route_ids, route_probs, w_gate, w_up, w_down):
    toks, width = tokens.shape
    local, _, hid = w_gate.shape
    half_w = width // 2
    rows = 16 * toks
    vmem = pl.BlockSpec(memory_space=pltpu.VMEM)
    hbm = pl.BlockSpec(memory_space=pl.ANY)
    scratch = [
        pltpu.VMEM((2, 2, 4, 2, 2, toks, width + LANES), BF16),
        pltpu.VMEM((width, 2 * local * hid), BF16),
        pltpu.VMEM((local, hid, width), BF16),
        pltpu.VMEM((rows, 2 * local * hid), F32),
        pltpu.VMEM((rows, local * hid), F32),
        pltpu.VMEM((rows, 2 * local * hid), BF16),
        pltpu.VMEM((2, 2, 2, 2, 4, toks, half_w), BF16),
        pltpu.VMEM((2, 2, 2, 4, toks, half_w), BF16),
        pltpu.VMEM((2, 2, 2, 4, toks, half_w), BF16),
        pltpu.VMEM((2, 4, toks, half_w), BF16),
        pltpu.VMEM((2, 4, toks, half_w), BF16),
        pltpu.VMEM((2, 4, toks, half_w), BF16),
        pltpu.VMEM((2, 4, toks, half_w), BF16),
        pltpu.VMEM((2, 4, toks, half_w), BF16),
        pltpu.VMEM((2, 3, toks, half_w), BF16),
        pltpu.SemaphoreType.DMA((COPIES,)),
        pltpu.SemaphoreType.DMA((COPIES,)),
        pltpu.SemaphoreType.DMA((2 * local + 1,)),
    ]
    flops = 2 * 2 * rows * width * local * hid * 5
    return pl.pallas_call(
        fused_kernel,
        out_shape=jax.ShapeDtypeStruct((toks, width), BF16),
        in_specs=[vmem, vmem, vmem, vmem, hbm, hbm, hbm],
        out_specs=vmem,
        scratch_shapes=scratch,
        compiler_params=pltpu.CompilerParams(
            collective_id=0, has_side_effects=True, vmem_limit_bytes=56 * 1024 * 1024
        ),
        cost_estimate=pl.CostEstimate(
            flops=flops, bytes_accessed=6 * local * hid * width, transcendentals=2 * rows * local * hid
        ),
    )(tokens, out_grad, route_ids, route_probs, w_gate, w_up, w_down)


def slot_matches(flat_ids, experts, capacity):
    onehot = (flat_ids[:, None] == jnp.arange(experts, dtype=jnp.int32)[None, :]).astype(jnp.int32)
    earlier = jnp.cumsum(onehot, axis=0) - onehot
    slot_rank = jnp.sum(earlier * onehot, axis=1)
    slot_of = flat_ids * capacity + slot_rank
    return slot_of[None, :] == jnp.arange(experts * capacity, dtype=jnp.int32)[:, None]


def select_matrix(matches, tok_count):
    return jnp.sum(matches.reshape(matches.shape[0], tok_count, TOPK).astype(jnp.float32), axis=2)


def build_tiles(token_rows, grad_rows, matches, flat_probs):
    select = select_matrix(matches, token_rows.shape[0]).astype(jnp.bfloat16)
    slot_scale = jnp.sum(jnp.where(matches, flat_probs[None, :], 0.0), axis=1)
    x_rows = jnp.dot(select, token_rows, preferred_element_type=jnp.float32).astype(jnp.bfloat16)
    g_rows = (
        jnp.dot(select, grad_rows, preferred_element_type=jnp.float32) * slot_scale[:, None]
    ).astype(jnp.bfloat16)
    return jnp.stack([x_rows, g_rows])


def expert_grads(tiles, w_gate, w_up, w_down):
    x_rows = tiles[:, 0]
    g_rows = tiles[:, 1]
    gate_pre = jnp.einsum("nsecd,edh->nsech", x_rows, w_gate, preferred_element_type=jnp.float32)
    up_pre = jnp.einsum("nsecd,edh->nsech", x_rows, w_up, preferred_element_type=jnp.float32)
    hidden_grad = jnp.einsum("nsecd,ehd->nsech", g_rows, w_down, preferred_element_type=jnp.float32)
    sigmoid_a = jax.nn.sigmoid(gate_pre)
    gate_grad = (hidden_grad * up_pre * sigmoid_a * (1.0 + gate_pre * (1.0 - sigmoid_a))).astype(
        jnp.bfloat16
    )
    up_grad = (hidden_grad * gate_pre * sigmoid_a).astype(jnp.bfloat16)
    partial_value = jnp.einsum(
        "nsech,edh->nsecd", gate_grad, w_gate, preferred_element_type=jnp.float32
    )
    partial_value = partial_value + jnp.einsum(
        "nsech,edh->nsecd", up_grad, w_up, preferred_element_type=jnp.float32
    )
    return partial_value.astype(jnp.bfloat16)


def on_device(tokens, out_grad, route_ids, route_probs, w_gate, w_up, w_down):
    columns = lax.axis_size("expert")
    local_experts = w_gate.shape[0]
    experts = local_experts * columns
    tok_count, width = tokens.shape
    capacity = max(2, 2 * tok_count * TOPK // experts)
    slots = experts * capacity
    tile_shape = (2, columns, local_experts, capacity, width)
    own_matches = slot_matches(route_ids.reshape(-1), experts, capacity)
    tiles = build_tiles(tokens, out_grad, own_matches, route_probs.reshape(-1)).reshape(
        (1,) + tile_shape
    )
    received = lax.all_to_all(tiles, "expert", split_axis=2, concat_axis=2, tiled=True)
    partials = expert_grads(
        lax.all_gather(received, "dp", axis=0, tiled=True), w_gate, w_up, w_down
    )
    summed = lax.psum_scatter(
        partials.astype(jnp.float32).astype(jnp.bfloat16), "dp", scatter_dimension=0, tiled=True
    ).astype(jnp.float32)
    returned = lax.all_to_all(
        summed.astype(jnp.bfloat16), "expert", split_axis=1, concat_axis=1, tiled=True
    ).astype(summed.dtype)
    own_select = select_matrix(own_matches, tok_count)
    result = jnp.dot(own_select.T, returned.reshape(slots, width), precision=lax.Precision.HIGHEST)
    return result.astype(jnp.bfloat16)


def solution(mesh):
    placed = (
        P(("dp", "expert"), None),
        P(("dp", "expert"), None),
        P(("dp", "expert"), None),
        P(("dp", "expert"), None),
        P("expert", None, "dp"),
        P("expert", None, "dp"),
        P("expert", "dp", None),
    )
    whole_block = dict(mesh.shape) == {"dp": 4, "expert": 8}

    def chosen(tokens, out_grad, route_ids, route_probs, w_gate, w_up, w_down):
        experts = w_gate.shape[0] * mesh.shape["expert"]
        dense = 2 * tokens.shape[0] * TOPK // experts >= tokens.shape[0]
        fits = tokens.shape[0] == 16 and experts <= LANES
        step = fused if whole_block and dense and fits else on_device
        return step(tokens, out_grad, route_ids, route_probs, w_gate, w_up, w_down)

    return jax.shard_map(
        chosen, mesh=mesh, in_specs=placed, out_specs=P(("dp", "expert"), None), check_vma=False
    )
```

```python
import jax
import jax.numpy as jnp
from jax import lax
from jax.experimental import pallas as pl
from jax.experimental.pallas import tpu as pltpu
from jax.sharding import PartitionSpec as P

TOPK = 8
LANES = 128
MESH = pl.DeviceIdType.MESH
BF16 = jnp.bfloat16
F32 = jnp.float32
COPIES = 80
NT = (((1,), (1,)), ((), ()))


def fused_kernel(
    tokens_ref, grads_ref, ids_ref, probs_ref, w_gate_ref, w_up_ref, w_down_ref, out_ref,
    rows_buf, w_cat, w_dn, acc_in, acc_hid, hid_grads, part, core_got, sum_a, sum_b,
    x_got, y_got, send2, got2, column, z_got, send_sems, recv_sems, local_sems,
):
    dp, ex = lax.axis_index("dp"), lax.axis_index("expert")
    y, x = dp // 2, dp % 2
    z, c = ex // 2, ex % 2
    oy, ox, oc = 1 - y, 1 - x, 1 - c
    to_x, to_y, to_core = (y * 2 + ox, ex), (oy * 2 + x, ex), (dp, z * 2 + oc)
    to_z = {k: (dp, ((z + k) % 4) * 2 + c) for k in (1, 2, 3)}
    toks, width = tokens_ref.shape
    half_w = width // 2
    local, _, hid = w_gate_ref.shape
    started = []

    def send(src, dst, device):
        at = len(started)
        copy = pltpu.make_async_remote_copy(
            src_ref=src, dst_ref=dst, send_sem=send_sems.at[at], recv_sem=recv_sems.at[at],
            device_id=device, device_id_type=MESH,
        )
        copy.start()
        started.append(copy)
        return copy

    barrier = pltpu.get_barrier_semaphore()
    for device in (to_x, to_y, to_core, to_z[1], to_z[2], to_z[3]):
        pl.semaphore_signal(barrier, inc=1, device_id=device, device_id_type=MESH)

    own = rows_buf.at[z, y, x, c]
    row_copies = [
        pltpu.make_async_copy(ref, own.at[n, :, pl.ds(0, width)], local_sems.at[n])
        for n, ref in enumerate((tokens_ref, grads_ref))
    ]
    weight_copies = []
    for e in range(local):
        for n, ref in enumerate((w_gate_ref, w_up_ref)):
            weight_copies.append(
                pltpu.make_async_copy(
                    ref.at[e],
                    w_cat.at[:, pl.ds((2 * e + n) * hid, hid)],
                    local_sems.at[2 + 2 * e + n],
                )
            )
    weight_copies.append(pltpu.make_async_copy(w_down_ref, w_dn, local_sems.at[2 + 2 * local]))
    for copy in row_copies + weight_copies:
        copy.start()

    expert = lax.broadcasted_iota(jnp.int32, (LANES, toks), 0)
    weights = jnp.zeros(expert.shape, F32)
    for k in range(TOPK):
        weights = weights + jnp.where(ids_ref[k : k + 1, :] == expert, probs_ref[k : k + 1, :], 0.0)
    high = weights.astype(BF16)
    low = (weights - high.astype(F32)).astype(BF16)
    diagonal = lax.broadcasted_iota(jnp.int32, (toks, toks), 0) == lax.broadcasted_iota(
        jnp.int32, (toks, toks), 1
    )
    eye = jnp.where(diagonal, 1.0, 0.0).astype(BF16)
    for copy in row_copies:
        copy.wait()
    for n, value in enumerate((high, low)):
        turned = lax.dot_general(eye, value, NT, preferred_element_type=F32)
        rows_buf[z, y, x, c, n, :, width:] = turned.astype(BF16)

    pl.semaphore_wait(barrier, 6)

    shifts = (0, 1, 3, 2)
    order = [(z + 4 - k) % 4 for k in shifts]
    x_in, y_in, z_in, diag_in = {}, {}, {}, {}
    core_in = {i: [] for i in range(4)}
    core_sum, stage1, stage2, z_out = {}, {}, {}, {}

    def to_plane(i):
        got = rows_buf.at[order[i], y, x, c]
        x_in[i] = send(got, got, to_x)
        y_in[i] = send(got, got, to_y)
        if i == 0:
            for k in shifts[1:]:
                z_in[k] = send(own, own, to_z[k])
        core_in[i].append(send(got, got, to_core))

    def from_z(i):
        z_in[shifts[i]].wait_recv()
        to_plane(i)

    def relay(i):
        x_in[i].wait_recv()
        got = rows_buf.at[order[i], y, ox, c]
        first = send(got.at[0], got.at[0], to_y)
        core_in[i].append(send(got, got, to_core))
        y_in[i].wait_recv()
        got = rows_buf.at[order[i], oy, x, c]
        diag_in[i] = (first, send(got.at[1], got.at[1], to_x))
        core_in[i].append(send(got, got, to_core))

    def share_diagonal(i):
        for n in range(2):
            diag_in[i][n].wait_recv()
            got = rows_buf.at[order[i], oy, ox, c, n]
            core_in[i].append(send(got, got, to_core))

    rows = 8 * toks
    k_tile = width // 2

    def compute(i):
        for copy in core_in[i]:
            copy.wait_recv()
        s = order[i]
        acc_in[...] = jnp.zeros_like(acc_in)
        acc_hid[...] = jnp.zeros_like(acc_hid)

        @pl.loop(0, width // k_tile)
        def _(k):
            cols = pl.ds(pl.multiple_of(k * k_tile, LANES), k_tile)
            x_rows = rows_buf[s, :, :, :, 0, :, cols].reshape(rows, k_tile)
            g_rows = rows_buf[s, :, :, :, 1, :, cols].reshape(rows, k_tile)
            acc_in[...] += jnp.dot(x_rows, w_cat[cols, :], preferred_element_type=F32)
            down = w_dn[:, :, cols].reshape(local * hid, k_tile)
            acc_hid[...] += lax.dot_general(g_rows, down, NT, preferred_element_type=F32)

        tail = pl.ds(width, LANES)
        wts = rows_buf[s, :, :, :, 0, :, tail].reshape(rows, LANES).astype(F32)
        wts = wts + rows_buf[s, :, :, :, 1, :, tail].reshape(rows, LANES).astype(F32)
        which = lax.broadcasted_iota(jnp.int32, (rows, LANES), 1)
        for e in range(local):
            scale = jnp.sum(jnp.where(which == ex * local + e, wts, 0.0), axis=1, keepdims=True)
            gate = acc_in[:, 2 * e * hid : (2 * e + 1) * hid]
            up = acc_in[:, (2 * e + 1) * hid : (2 * e + 2) * hid]
            grad = acc_hid[:, e * hid : (e + 1) * hid] * scale
            sig = jax.nn.sigmoid(gate)
            hid_grads[:, 2 * e * hid : (2 * e + 1) * hid] = (
                grad * up * sig * (1.0 + gate * (1.0 - sig))
            ).astype(BF16)
            hid_grads[:, (2 * e + 1) * hid : (2 * e + 2) * hid] = (grad * gate * sig).astype(BF16)
        for half in range(2):
            w_rows = pl.ds(half * half_w, half_w)
            value = lax.dot_general(hid_grads[...], w_cat[w_rows, :], NT, preferred_element_type=F32)
            value = value.astype(BF16).reshape(2, 2, 2, toks, half_w)
            part[i, half, 0] = value[:, :, 0]
            part[i, half, 1] = value[:, :, 1]
            core_sum[i, half] = send(part.at[i, half, oc], core_got.at[i, half], to_core)

    def add(*refs):
        total = refs[0][...].astype(F32)
        for ref in refs[1:]:
            total = total + ref[...].astype(F32)
        return total.astype(BF16)

    def reduce1(i):
        core_sum[i, 0].wait_recv()
        for by in range(2):
            for bx in range(2):
                sum_a[i, bx, by] = add(part.at[i, 0, c, by, bx], core_got.at[i, 0, by, bx])
        first = send(sum_a.at[i, ox], x_got.at[i], to_x)
        core_sum[i, 1].wait_recv()
        for by in range(2):
            for bx in range(2):
                sum_b[i, by, bx] = add(part.at[i, 1, c, by, bx], core_got.at[i, 1, by, bx])
        stage1[i] = (first, send(sum_b.at[i, oy], y_got.at[i], to_y))

    def reduce2(i):
        stage1[i][0].wait_recv()
        send2[i, 0] = add(sum_a.at[i, x, oy], x_got.at[i, oy])
        first = send(send2.at[i, 0], got2.at[i, 0], to_y)
        stage1[i][1].wait_recv()
        send2[i, 1] = add(sum_b.at[i, y, ox], y_got.at[i, ox])
        stage2[i] = (first, send(send2.at[i, 1], got2.at[i, 1], to_x))

    def reduce3(i):
        stage2[i][0].wait_recv()
        column[i, 0] = add(sum_a.at[i, x, y], x_got.at[i, y], got2.at[i, 0])
        stage2[i][1].wait_recv()
        column[i, 1] = add(sum_b.at[i, y, x], y_got.at[i, x], got2.at[i, 1])
        if i > 0:
            z_out[i] = send(column.at[i], z_got.at[i - 1], to_z[4 - shifts[i]])

    to_plane(0)
    from_z(1)
    relay(0)
    from_z(2)
    relay(1)
    share_diagonal(0)
    for copy in weight_copies:
        copy.wait()
    compute(0)
    from_z(3)
    relay(2)
    share_diagonal(1)
    reduce1(0)
    compute(1)
    relay(3)
    share_diagonal(2)
    reduce1(1)
    reduce2(0)
    compute(2)
    share_diagonal(3)
    reduce1(2)
    reduce2(1)
    reduce3(0)
    compute(3)
    reduce1(3)
    reduce2(2)
    reduce3(1)
    reduce2(3)
    reduce3(2)
    reduce3(3)
    for i in (1, 2, 3):
        z_out[i].wait_recv()
    for half in range(2):
        out_ref[:, half * half_w : (half + 1) * half_w] = add(
            column.at[0, half], z_got.at[0, half], z_got.at[1, half], z_got.at[2, half]
        )
    for copy in started:
        copy.wait_send()


def fused(tokens, out_grad, route_ids, route_probs, w_gate, w_up, w_down):
    toks, width = tokens.shape
    local, _, hid = w_gate.shape
    half_w = width // 2
    rows = 8 * toks
    vmem = pl.BlockSpec(memory_space=pltpu.VMEM)
    hbm = pl.BlockSpec(memory_space=pl.ANY)
    scratch = [
        pltpu.VMEM((4, 2, 2, 2, 2, toks, width + LANES), BF16),
        pltpu.VMEM((width, 2 * local * hid), BF16),
        pltpu.VMEM((local, hid, width), BF16),
        pltpu.VMEM((rows, 2 * local * hid), F32),
        pltpu.VMEM((rows, local * hid), F32),
        pltpu.VMEM((rows, 2 * local * hid), BF16),
        pltpu.VMEM((4, 2, 2, 2, 2, toks, half_w), BF16),
        pltpu.VMEM((4, 2, 2, 2, toks, half_w), BF16),
        pltpu.VMEM((4, 2, 2, toks, half_w), BF16),
        pltpu.VMEM((4, 2, 2, toks, half_w), BF16),
        pltpu.VMEM((4, 2, toks, half_w), BF16),
        pltpu.VMEM((4, 2, toks, half_w), BF16),
        pltpu.VMEM((4, 2, toks, half_w), BF16),
        pltpu.VMEM((4, 2, toks, half_w), BF16),
        pltpu.VMEM((4, 2, toks, half_w), BF16),
        pltpu.VMEM((3, 2, toks, half_w), BF16),
        pltpu.SemaphoreType.DMA((COPIES,)),
        pltpu.SemaphoreType.DMA((COPIES,)),
        pltpu.SemaphoreType.DMA((2 * local + 3,)),
    ]
    flops = 2 * 4 * rows * width * local * hid * 5
    return pl.pallas_call(
        fused_kernel,
        out_shape=jax.ShapeDtypeStruct((toks, width), BF16),
        in_specs=[hbm, hbm, vmem, vmem, hbm, hbm, hbm],
        out_specs=vmem,
        scratch_shapes=scratch,
        compiler_params=pltpu.CompilerParams(
            collective_id=0, has_side_effects=True, vmem_limit_bytes=56 * 1024 * 1024
        ),
        cost_estimate=pl.CostEstimate(
            flops=flops, bytes_accessed=6 * local * hid * width, transcendentals=4 * rows * local * hid
        ),
    )(tokens, out_grad, route_ids.T, route_probs.T, w_gate, w_up, w_down)


def slot_matches(flat_ids, experts, capacity):
    onehot = (flat_ids[:, None] == jnp.arange(experts, dtype=jnp.int32)[None, :]).astype(jnp.int32)
    earlier = jnp.cumsum(onehot, axis=0) - onehot
    slot_rank = jnp.sum(earlier * onehot, axis=1)
    slot_of = flat_ids * capacity + slot_rank
    return slot_of[None, :] == jnp.arange(experts * capacity, dtype=jnp.int32)[:, None]


def select_matrix(matches, tok_count):
    return jnp.sum(matches.reshape(matches.shape[0], tok_count, TOPK).astype(jnp.float32), axis=2)


def build_tiles(token_rows, grad_rows, matches, flat_probs):
    select = select_matrix(matches, token_rows.shape[0]).astype(jnp.bfloat16)
    slot_scale = jnp.sum(jnp.where(matches, flat_probs[None, :], 0.0), axis=1)
    x_rows = jnp.dot(select, token_rows, preferred_element_type=jnp.float32).astype(jnp.bfloat16)
    g_rows = (
        jnp.dot(select, grad_rows, preferred_element_type=jnp.float32) * slot_scale[:, None]
    ).astype(jnp.bfloat16)
    return jnp.stack([x_rows, g_rows])


def expert_grads(tiles, w_gate, w_up, w_down):
    x_rows = tiles[:, 0]
    g_rows = tiles[:, 1]
    gate_pre = jnp.einsum("nsecd,edh->nsech", x_rows, w_gate, preferred_element_type=jnp.float32)
    up_pre = jnp.einsum("nsecd,edh->nsech", x_rows, w_up, preferred_element_type=jnp.float32)
    hidden_grad = jnp.einsum("nsecd,ehd->nsech", g_rows, w_down, preferred_element_type=jnp.float32)
    sigmoid_a = jax.nn.sigmoid(gate_pre)
    gate_grad = (hidden_grad * up_pre * sigmoid_a * (1.0 + gate_pre * (1.0 - sigmoid_a))).astype(
        jnp.bfloat16
    )
    up_grad = (hidden_grad * gate_pre * sigmoid_a).astype(jnp.bfloat16)
    partial_value = jnp.einsum(
        "nsech,edh->nsecd", gate_grad, w_gate, preferred_element_type=jnp.float32
    )
    partial_value = partial_value + jnp.einsum(
        "nsech,edh->nsecd", up_grad, w_up, preferred_element_type=jnp.float32
    )
    return partial_value.astype(jnp.bfloat16)


def on_device(tokens, out_grad, route_ids, route_probs, w_gate, w_up, w_down):
    columns = lax.axis_size("expert")
    local_experts = w_gate.shape[0]
    experts = local_experts * columns
    tok_count, width = tokens.shape
    capacity = max(2, 2 * tok_count * TOPK // experts)
    slots = experts * capacity
    tile_shape = (2, columns, local_experts, capacity, width)
    own_matches = slot_matches(route_ids.reshape(-1), experts, capacity)
    tiles = build_tiles(tokens, out_grad, own_matches, route_probs.reshape(-1)).reshape(
        (1,) + tile_shape
    )
    received = lax.all_to_all(tiles, "expert", split_axis=2, concat_axis=2, tiled=True)
    partials = expert_grads(
        lax.all_gather(received, "dp", axis=0, tiled=True), w_gate, w_up, w_down
    )
    summed = lax.psum_scatter(
        partials.astype(jnp.float32).astype(jnp.bfloat16), "dp", scatter_dimension=0, tiled=True
    ).astype(jnp.float32)
    returned = lax.all_to_all(
        summed.astype(jnp.bfloat16), "expert", split_axis=1, concat_axis=1, tiled=True
    ).astype(summed.dtype)
    own_select = select_matrix(own_matches, tok_count)
    result = jnp.dot(own_select.T, returned.reshape(slots, width), precision=lax.Precision.HIGHEST)
    return result.astype(jnp.bfloat16)


def solution(mesh):
    placed = (
        P(("dp", "expert"), None),
        P(("dp", "expert"), None),
        P(("dp", "expert"), None),
        P(("dp", "expert"), None),
        P("expert", None, "dp"),
        P("expert", None, "dp"),
        P("expert", "dp", None),
    )
    whole_block = dict(mesh.shape) == {"dp": 4, "expert": 8}

    def chosen(tokens, out_grad, route_ids, route_probs, w_gate, w_up, w_down):
        experts = w_gate.shape[0] * mesh.shape["expert"]
        dense = 2 * tokens.shape[0] * TOPK // experts >= tokens.shape[0]
        fits = tokens.shape[0] == 16 and experts <= LANES
        step = fused if whole_block and dense and fits else on_device
        return step(tokens, out_grad, route_ids, route_probs, w_gate, w_up, w_down)

    return jax.shard_map(
        chosen, mesh=mesh, in_specs=placed, out_specs=P(("dp", "expert"), None), check_vma=False
    )
```

```python
import jax
import jax.numpy as jnp
from jax import lax
from jax.experimental import pallas as pl
from jax.experimental.pallas import tpu as pltpu
from jax.sharding import PartitionSpec as P

TOPK = 8
LANES = 128
MESH = pl.DeviceIdType.MESH
BF16 = jnp.bfloat16
F32 = jnp.float32
COPIES = 80
NT = (((1,), (1,)), ((), ()))


def fused_kernel(
    tokens_ref, grads_ref, ids_ref, probs_ref, w_gate_ref, w_up_ref, w_down_ref, out_ref,
    rows_buf, w_cat, w_dn, acc_in, acc_hid, hid_grads, part, core_got, sum_a, sum_b,
    x_got, y_got, send2, got2, column, z_got, send_sems, recv_sems, z_send_sems, z_recv_sems, local_sems,
):
    dp, ex = lax.axis_index("dp"), lax.axis_index("expert")
    y, x = dp // 2, dp % 2
    z, c = ex // 2, ex % 2
    oy, ox, oc = 1 - y, 1 - x, 1 - c
    to_x, to_y, to_core = (y * 2 + ox, ex), (oy * 2 + x, ex), (dp, z * 2 + oc)
    to_z = {k: (dp, ((z + k) % 4) * 2 + c) for k in (1, 2, 3)}
    toks, width = tokens_ref.shape
    half_w = width // 2
    local, _, hid = w_gate_ref.shape
    started = []

    def send(src, dst, device):
        at = len(started)
        copy = pltpu.make_async_remote_copy(
            src_ref=src, dst_ref=dst, send_sem=send_sems.at[at], recv_sem=recv_sems.at[at],
            device_id=device, device_id_type=MESH,
        )
        copy.start()
        started.append(copy)
        return copy

    barrier = pltpu.get_barrier_semaphore()
    for device in (to_x, to_y, to_core, to_z[1], to_z[2], to_z[3]):
        pl.semaphore_signal(barrier, inc=1, device_id=device, device_id_type=MESH)

    own = rows_buf.at[z, y, x, c]
    row_copies = [
        pltpu.make_async_copy(ref, own.at[n, :, pl.ds(0, width)], local_sems.at[n])
        for n, ref in enumerate((tokens_ref, grads_ref))
    ]
    weight_copies = []
    for e in range(local):
        for n, ref in enumerate((w_gate_ref, w_up_ref)):
            weight_copies.append(
                pltpu.make_async_copy(
                    ref.at[e],
                    w_cat.at[:, pl.ds((2 * e + n) * hid, hid)],
                    local_sems.at[2 + 2 * e + n],
                )
            )
    weight_copies.append(pltpu.make_async_copy(w_down_ref, w_dn, local_sems.at[2 + 2 * local]))
    for copy in row_copies + weight_copies:
        copy.start()

    expert = lax.broadcasted_iota(jnp.int32, (LANES, toks), 0)
    weights = jnp.zeros(expert.shape, F32)
    for k in range(TOPK):
        weights = weights + jnp.where(ids_ref[k : k + 1, :] == expert, probs_ref[k : k + 1, :], 0.0)
    high = weights.astype(BF16)
    low = (weights - high.astype(F32)).astype(BF16)
    diagonal = lax.broadcasted_iota(jnp.int32, (toks, toks), 0) == lax.broadcasted_iota(
        jnp.int32, (toks, toks), 1
    )
    eye = jnp.where(diagonal, 1.0, 0.0).astype(BF16)
    for copy in row_copies:
        copy.wait()
    for n, value in enumerate((high, low)):
        turned = lax.dot_general(eye, value, NT, preferred_element_type=F32)
        rows_buf[z, y, x, c, n, :, width:] = turned.astype(BF16)

    pl.semaphore_wait(barrier, 6)

    upper = z // 2
    inner = z + upper * (3 - 2 * z)
    order = [z] + [f + upper * (3 - 2 * f) for f in (1 - inner, 2, 3)]
    x_in, y_in, diag_in = {}, {}, {}
    z_sent = []
    core_in = {i: [] for i in range(4)}
    core_sum, stage1, stage2 = {}, {}, {}

    def z_copy(src, dst, target, source, kind, at):
        return pltpu.make_async_remote_copy(
            src_ref=src, dst_ref=dst, send_sem=z_send_sems.at[kind, at],
            recv_sem=z_recv_sems.at[kind, source],
            device_id=(dp, target * 2 + c), device_id_type=MESH,
        )

    def along_z(source, target, at):
        got = rows_buf.at[source, y, x, c]
        copy = z_copy(got, got, target, source, 0, at)
        there = jnp.logical_and(target >= 0, target <= 3)

        @pl.when(there)
        def _():
            copy.start()

        z_sent.append((copy, there))

    def to_plane(i):
        got = rows_buf.at[order[i], y, x, c]
        x_in[i] = send(got, got, to_x)
        y_in[i] = send(got, got, to_y)
        if i == 0:
            along_z(z, z - 1, 0)
            along_z(z, z + 1, 4)
        core_in[i].append(send(got, got, to_core))

    def from_z(i):
        s = order[i]
        got = rows_buf.at[s, y, x, c]
        z_copy(got, got, s, s, 0, 0).wait_recv()
        up = (z + 4 - s) // 4
        along_z(s, z + 2 * up - 1, i)
        to_plane(i)

    def relay(i):
        x_in[i].wait_recv()
        got = rows_buf.at[order[i], y, ox, c]
        first = send(got.at[0], got.at[0], to_y)
        core_in[i].append(send(got, got, to_core))
        y_in[i].wait_recv()
        got = rows_buf.at[order[i], oy, x, c]
        diag_in[i] = (first, send(got.at[1], got.at[1], to_x))
        core_in[i].append(send(got, got, to_core))

    def share_diagonal(i):
        for n in range(2):
            diag_in[i][n].wait_recv()
            got = rows_buf.at[order[i], oy, ox, c, n]
            core_in[i].append(send(got, got, to_core))

    rows = 8 * toks
    k_tile = width // 2

    def compute(i):
        for copy in core_in[i]:
            copy.wait_recv()
        s = order[i]
        acc_in[...] = jnp.zeros_like(acc_in)
        acc_hid[...] = jnp.zeros_like(acc_hid)

        @pl.loop(0, width // k_tile)
        def _(k):
            cols = pl.ds(pl.multiple_of(k * k_tile, LANES), k_tile)
            x_rows = rows_buf[s, :, :, :, 0, :, cols].reshape(rows, k_tile)
            g_rows = rows_buf[s, :, :, :, 1, :, cols].reshape(rows, k_tile)
            acc_in[...] += jnp.dot(x_rows, w_cat[cols, :], preferred_element_type=F32)
            down = w_dn[:, :, cols].reshape(local * hid, k_tile)
            acc_hid[...] += lax.dot_general(g_rows, down, NT, preferred_element_type=F32)

        tail = pl.ds(width, LANES)
        wts = rows_buf[s, :, :, :, 0, :, tail].reshape(rows, LANES).astype(F32)
        wts = wts + rows_buf[s, :, :, :, 1, :, tail].reshape(rows, LANES).astype(F32)
        which = lax.broadcasted_iota(jnp.int32, (rows, LANES), 1)
        for e in range(local):
            scale = jnp.sum(jnp.where(which == ex * local + e, wts, 0.0), axis=1, keepdims=True)
            gate = acc_in[:, 2 * e * hid : (2 * e + 1) * hid]
            up = acc_in[:, (2 * e + 1) * hid : (2 * e + 2) * hid]
            grad = acc_hid[:, e * hid : (e + 1) * hid] * scale
            sig = jax.nn.sigmoid(gate)
            hid_grads[:, 2 * e * hid : (2 * e + 1) * hid] = (
                grad * up * sig * (1.0 + gate * (1.0 - sig))
            ).astype(BF16)
            hid_grads[:, (2 * e + 1) * hid : (2 * e + 2) * hid] = (grad * gate * sig).astype(BF16)
        for half in range(2):
            w_rows = pl.ds(half * half_w, half_w)
            value = lax.dot_general(hid_grads[...], w_cat[w_rows, :], NT, preferred_element_type=F32)
            value = value.astype(BF16).reshape(2, 2, 2, toks, half_w)
            part[i, half, 0] = value[:, :, 0]
            part[i, half, 1] = value[:, :, 1]
            core_sum[i, half] = send(part.at[i, half, oc], core_got.at[i, half], to_core)

    def add(*refs):
        total = refs[0][...].astype(F32)
        for ref in refs[1:]:
            total = total + ref[...].astype(F32)
        return total.astype(BF16)

    def reduce1(i):
        core_sum[i, 0].wait_recv()
        for by in range(2):
            for bx in range(2):
                sum_a[i, bx, by] = add(part.at[i, 0, c, by, bx], core_got.at[i, 0, by, bx])
        first = send(sum_a.at[i, ox], x_got.at[i], to_x)
        core_sum[i, 1].wait_recv()
        for by in range(2):
            for bx in range(2):
                sum_b[i, by, bx] = add(part.at[i, 1, c, by, bx], core_got.at[i, 1, by, bx])
        stage1[i] = (first, send(sum_b.at[i, oy], y_got.at[i], to_y))

    def reduce2(i):
        stage1[i][0].wait_recv()
        send2[i, 0] = add(sum_a.at[i, x, oy], x_got.at[i, oy])
        first = send(send2.at[i, 0], got2.at[i, 0], to_y)
        stage1[i][1].wait_recv()
        send2[i, 1] = add(sum_b.at[i, y, ox], y_got.at[i, ox])
        stage2[i] = (first, send(send2.at[i, 1], got2.at[i, 1], to_x))

    def reduce3(i):
        stage2[i][0].wait_recv()
        column[i, 0] = add(sum_a.at[i, x, y], x_got.at[i, y], got2.at[i, 0])
        stage2[i][1].wait_recv()
        column[i, 1] = add(sum_b.at[i, y, x], y_got.at[i, x], got2.at[i, 1])
        if i > 0:
            copy = z_copy(column.at[i], z_got.at[z], order[i], z, 1, i)
            copy.start()
            z_sent.append((copy, None))

    to_plane(0)
    from_z(1)
    relay(0)
    from_z(2)
    relay(1)
    share_diagonal(0)
    for copy in weight_copies:
        copy.wait()
    compute(0)
    from_z(3)
    relay(2)
    share_diagonal(1)
    reduce1(0)
    compute(1)
    relay(3)
    share_diagonal(2)
    reduce1(1)
    reduce2(0)
    compute(2)
    share_diagonal(3)
    reduce1(2)
    reduce2(1)
    reduce3(0)
    compute(3)
    reduce1(3)
    reduce2(2)
    reduce3(1)
    reduce2(3)
    reduce3(2)
    reduce3(3)
    for s in order[1:]:
        got = z_got.at[s]
        z_copy(got, got, s, s, 1, 0).wait_recv()
    for half in range(2):
        out_ref[:, half * half_w : (half + 1) * half_w] = add(
            column.at[0, half], *[z_got.at[s, half] for s in order[1:]]
        )
    for copy in started:
        copy.wait_send()
    for copy, there in z_sent:
        if there is None:
            copy.wait_send()
        else:

            @pl.when(there)
            def _(copy=copy):
                copy.wait_send()


def fused(tokens, out_grad, route_ids, route_probs, w_gate, w_up, w_down):
    toks, width = tokens.shape
    local, _, hid = w_gate.shape
    half_w = width // 2
    rows = 8 * toks
    vmem = pl.BlockSpec(memory_space=pltpu.VMEM)
    hbm = pl.BlockSpec(memory_space=pl.ANY)
    scratch = [
        pltpu.VMEM((4, 2, 2, 2, 2, toks, width + LANES), BF16),
        pltpu.VMEM((width, 2 * local * hid), BF16),
        pltpu.VMEM((local, hid, width), BF16),
        pltpu.VMEM((rows, 2 * local * hid), F32),
        pltpu.VMEM((rows, local * hid), F32),
        pltpu.VMEM((rows, 2 * local * hid), BF16),
        pltpu.VMEM((4, 2, 2, 2, 2, toks, half_w), BF16),
        pltpu.VMEM((4, 2, 2, 2, toks, half_w), BF16),
        pltpu.VMEM((4, 2, 2, toks, half_w), BF16),
        pltpu.VMEM((4, 2, 2, toks, half_w), BF16),
        pltpu.VMEM((4, 2, toks, half_w), BF16),
        pltpu.VMEM((4, 2, toks, half_w), BF16),
        pltpu.VMEM((4, 2, toks, half_w), BF16),
        pltpu.VMEM((4, 2, toks, half_w), BF16),
        pltpu.VMEM((4, 2, toks, half_w), BF16),
        pltpu.VMEM((4, 2, toks, half_w), BF16),
        pltpu.SemaphoreType.DMA((COPIES,)),
        pltpu.SemaphoreType.DMA((COPIES,)),
        pltpu.SemaphoreType.DMA((2, 5)),
        pltpu.SemaphoreType.DMA((2, 4)),
        pltpu.SemaphoreType.DMA((2 * local + 3,)),
    ]
    flops = 2 * 4 * rows * width * local * hid * 5
    return pl.pallas_call(
        fused_kernel,
        out_shape=jax.ShapeDtypeStruct((toks, width), BF16),
        in_specs=[hbm, hbm, vmem, vmem, hbm, hbm, hbm],
        out_specs=vmem,
        scratch_shapes=scratch,
        compiler_params=pltpu.CompilerParams(
            collective_id=0, has_side_effects=True, vmem_limit_bytes=56 * 1024 * 1024
        ),
        cost_estimate=pl.CostEstimate(
            flops=flops, bytes_accessed=6 * local * hid * width, transcendentals=4 * rows * local * hid
        ),
    )(tokens, out_grad, route_ids.T, route_probs.T, w_gate, w_up, w_down)


def slot_matches(flat_ids, experts, capacity):
    onehot = (flat_ids[:, None] == jnp.arange(experts, dtype=jnp.int32)[None, :]).astype(jnp.int32)
    earlier = jnp.cumsum(onehot, axis=0) - onehot
    slot_rank = jnp.sum(earlier * onehot, axis=1)
    slot_of = flat_ids * capacity + slot_rank
    return slot_of[None, :] == jnp.arange(experts * capacity, dtype=jnp.int32)[:, None]


def select_matrix(matches, tok_count):
    return jnp.sum(matches.reshape(matches.shape[0], tok_count, TOPK).astype(jnp.float32), axis=2)


def build_tiles(token_rows, grad_rows, matches, flat_probs):
    select = select_matrix(matches, token_rows.shape[0]).astype(jnp.bfloat16)
    slot_scale = jnp.sum(jnp.where(matches, flat_probs[None, :], 0.0), axis=1)
    x_rows = jnp.dot(select, token_rows, preferred_element_type=jnp.float32).astype(jnp.bfloat16)
    g_rows = (
        jnp.dot(select, grad_rows, preferred_element_type=jnp.float32) * slot_scale[:, None]
    ).astype(jnp.bfloat16)
    return jnp.stack([x_rows, g_rows])


def expert_grads(tiles, w_gate, w_up, w_down):
    x_rows = tiles[:, 0]
    g_rows = tiles[:, 1]
    gate_pre = jnp.einsum("nsecd,edh->nsech", x_rows, w_gate, preferred_element_type=jnp.float32)
    up_pre = jnp.einsum("nsecd,edh->nsech", x_rows, w_up, preferred_element_type=jnp.float32)
    hidden_grad = jnp.einsum("nsecd,ehd->nsech", g_rows, w_down, preferred_element_type=jnp.float32)
    sigmoid_a = jax.nn.sigmoid(gate_pre)
    gate_grad = (hidden_grad * up_pre * sigmoid_a * (1.0 + gate_pre * (1.0 - sigmoid_a))).astype(
        jnp.bfloat16
    )
    up_grad = (hidden_grad * gate_pre * sigmoid_a).astype(jnp.bfloat16)
    partial_value = jnp.einsum(
        "nsech,edh->nsecd", gate_grad, w_gate, preferred_element_type=jnp.float32
    )
    partial_value = partial_value + jnp.einsum(
        "nsech,edh->nsecd", up_grad, w_up, preferred_element_type=jnp.float32
    )
    return partial_value.astype(jnp.bfloat16)


def on_device(tokens, out_grad, route_ids, route_probs, w_gate, w_up, w_down):
    columns = lax.axis_size("expert")
    local_experts = w_gate.shape[0]
    experts = local_experts * columns
    tok_count, width = tokens.shape
    capacity = max(2, 2 * tok_count * TOPK // experts)
    slots = experts * capacity
    tile_shape = (2, columns, local_experts, capacity, width)
    own_matches = slot_matches(route_ids.reshape(-1), experts, capacity)
    tiles = build_tiles(tokens, out_grad, own_matches, route_probs.reshape(-1)).reshape(
        (1,) + tile_shape
    )
    received = lax.all_to_all(tiles, "expert", split_axis=2, concat_axis=2, tiled=True)
    partials = expert_grads(
        lax.all_gather(received, "dp", axis=0, tiled=True), w_gate, w_up, w_down
    )
    summed = lax.psum_scatter(
        partials.astype(jnp.float32).astype(jnp.bfloat16), "dp", scatter_dimension=0, tiled=True
    ).astype(jnp.float32)
    returned = lax.all_to_all(
        summed.astype(jnp.bfloat16), "expert", split_axis=1, concat_axis=1, tiled=True
    ).astype(summed.dtype)
    own_select = select_matrix(own_matches, tok_count)
    result = jnp.dot(own_select.T, returned.reshape(slots, width), precision=lax.Precision.HIGHEST)
    return result.astype(jnp.bfloat16)


def solution(mesh):
    placed = (
        P(("dp", "expert"), None),
        P(("dp", "expert"), None),
        P(("dp", "expert"), None),
        P(("dp", "expert"), None),
        P("expert", None, "dp"),
        P("expert", None, "dp"),
        P("expert", "dp", None),
    )
    whole_block = dict(mesh.shape) == {"dp": 4, "expert": 8}

    def chosen(tokens, out_grad, route_ids, route_probs, w_gate, w_up, w_down):
        experts = w_gate.shape[0] * mesh.shape["expert"]
        dense = 2 * tokens.shape[0] * TOPK // experts >= tokens.shape[0]
        fits = tokens.shape[0] == 16 and experts <= LANES
        step = fused if whole_block and dense and fits else on_device
        return step(tokens, out_grad, route_ids, route_probs, w_gate, w_up, w_down)

    return jax.shard_map(
        chosen, mesh=mesh, in_specs=placed, out_specs=P(("dp", "expert"), None), check_vma=False
    )
```

```python
import jax
import jax.numpy as jnp
from jax import lax
from jax.experimental import pallas as pl
from jax.experimental.pallas import tpu as pltpu
from jax.sharding import PartitionSpec as P

TOPK = 8
LANES = 128
MESH = pl.DeviceIdType.MESH
BF16 = jnp.bfloat16
F32 = jnp.float32
COPIES = 80
NT = (((1,), (1,)), ((), ()))


def fused_kernel(
    tokens_ref, grads_ref, ids_ref, probs_ref, w_gate_ref, w_up_ref, w_down_ref, out_ref,
    rows_buf, w_cat, w_dn, w_cat_t, w_dn_t, acc_in, acc_hid, hid_grads, part, core_got, sum_a, sum_b,
    x_got, y_got, send2, got2, column, z_got, send_sems, recv_sems, z_send_sems, z_recv_sems, local_sems,
):
    dp, ex = lax.axis_index("dp"), lax.axis_index("expert")
    y, x = dp // 2, dp % 2
    z, c = ex // 2, ex % 2
    oy, ox, oc = 1 - y, 1 - x, 1 - c
    to_x, to_y, to_core = (y * 2 + ox, ex), (oy * 2 + x, ex), (dp, z * 2 + oc)
    to_z = {k: (dp, ((z + k) % 4) * 2 + c) for k in (1, 2, 3)}
    toks, width = tokens_ref.shape
    half_w = width // 2
    local, _, hid = w_gate_ref.shape
    started = []

    def send(src, dst, device):
        at = len(started)
        copy = pltpu.make_async_remote_copy(
            src_ref=src, dst_ref=dst, send_sem=send_sems.at[at], recv_sem=recv_sems.at[at],
            device_id=device, device_id_type=MESH,
        )
        copy.start()
        started.append(copy)
        return copy

    barrier = pltpu.get_barrier_semaphore()
    for device in (to_x, to_y, to_core, to_z[1], to_z[2], to_z[3]):
        pl.semaphore_signal(barrier, inc=1, device_id=device, device_id_type=MESH)

    own = rows_buf.at[z, y, x, c]
    row_copies = [
        pltpu.make_async_copy(ref, own.at[n, :, pl.ds(0, width)], local_sems.at[n])
        for n, ref in enumerate((tokens_ref, grads_ref))
    ]
    weight_copies = []
    for e in range(local):
        for n, ref in enumerate((w_gate_ref, w_up_ref)):
            weight_copies.append(
                pltpu.make_async_copy(
                    ref.at[e],
                    w_cat.at[:, pl.ds((2 * e + n) * hid, hid)],
                    local_sems.at[2 + 2 * e + n],
                )
            )
    weight_copies.insert(0, pltpu.make_async_copy(w_down_ref, w_dn, local_sems.at[2 + 2 * local]))
    for copy in row_copies + weight_copies:
        copy.start()

    expert = lax.broadcasted_iota(jnp.int32, (LANES, toks), 0)
    weights = jnp.zeros(expert.shape, F32)
    for k in range(TOPK):
        weights = weights + jnp.where(ids_ref[k : k + 1, :] == expert, probs_ref[k : k + 1, :], 0.0)
    high = weights.astype(BF16)
    low = (weights - high.astype(F32)).astype(BF16)
    diagonal = lax.broadcasted_iota(jnp.int32, (toks, toks), 0) == lax.broadcasted_iota(
        jnp.int32, (toks, toks), 1
    )
    eye = jnp.where(diagonal, 1.0, 0.0).astype(BF16)
    for copy in row_copies:
        copy.wait()
    for n, value in enumerate((high, low)):
        turned = lax.dot_general(eye, value, NT, preferred_element_type=F32)
        rows_buf[z, y, x, c, n, :, width:] = turned.astype(BF16)

    pl.semaphore_wait(barrier, 6)

    upper = z // 2
    inner = z + upper * (3 - 2 * z)
    order = [z] + [f + upper * (3 - 2 * f) for f in (1 - inner, 2, 3)]
    x_in, y_in, diag_in = {}, {}, {}
    z_sent = []
    core_in = {i: [] for i in range(4)}
    core_sum, stage1, stage2 = {}, {}, {}

    def z_copy(src, dst, target, source, kind, at):
        return pltpu.make_async_remote_copy(
            src_ref=src, dst_ref=dst, send_sem=z_send_sems.at[kind, at],
            recv_sem=z_recv_sems.at[kind, source],
            device_id=(dp, target * 2 + c), device_id_type=MESH,
        )

    def along_z(source, target, at):
        got = rows_buf.at[source, y, x, c]
        copy = z_copy(got, got, target, source, 0, at)
        there = jnp.logical_and(target >= 0, target <= 3)

        @pl.when(there)
        def _():
            copy.start()

        z_sent.append((copy, there))

    def to_plane(i):
        got = rows_buf.at[order[i], y, x, c]
        x_in[i] = send(got, got, to_x)
        y_in[i] = send(got, got, to_y)
        if i == 0:
            along_z(z, z - 1, 0)
            along_z(z, z + 1, 4)
        core_in[i].append(send(got, got, to_core))

    def from_z(i):
        s = order[i]
        got = rows_buf.at[s, y, x, c]
        z_copy(got, got, s, s, 0, 0).wait_recv()
        up = (z + 4 - s) // 4
        along_z(s, z + 2 * up - 1, i)
        to_plane(i)

    def relay(i):
        x_in[i].wait_recv()
        got = rows_buf.at[order[i], y, ox, c]
        first = send(got.at[0], got.at[0], to_y)
        core_in[i].append(send(got, got, to_core))
        y_in[i].wait_recv()
        got = rows_buf.at[order[i], oy, x, c]
        diag_in[i] = (first, send(got.at[1], got.at[1], to_x))
        core_in[i].append(send(got, got, to_core))

    def share_diagonal(i):
        for n in range(2):
            diag_in[i][n].wait_recv()
            got = rows_buf.at[order[i], oy, ox, c, n]
            core_in[i].append(send(got, got, to_core))

    rows = 8 * toks
    k_tile = width // 2

    def compute(i):
        for copy in core_in[i]:
            copy.wait_recv()
        s = order[i]
        acc_in[...] = jnp.zeros_like(acc_in)
        acc_hid[...] = jnp.zeros_like(acc_hid)

        @pl.loop(0, width // k_tile)
        def _(k):
            cols = pl.ds(pl.multiple_of(k * k_tile, LANES), k_tile)
            x_rows = rows_buf[s, :, :, :, 0, :, cols].reshape(rows, k_tile)
            g_rows = rows_buf[s, :, :, :, 1, :, cols].reshape(rows, k_tile)
            acc_in[...] += jnp.dot(x_rows, w_cat[cols, :], preferred_element_type=F32)
            acc_hid[...] += jnp.dot(g_rows, w_dn_t[cols, :], preferred_element_type=F32)

        tail = pl.ds(width, LANES)
        wts = rows_buf[s, :, :, :, 0, :, tail].reshape(rows, LANES).astype(F32)
        wts = wts + rows_buf[s, :, :, :, 1, :, tail].reshape(rows, LANES).astype(F32)
        which = lax.broadcasted_iota(jnp.int32, (rows, LANES), 1)
        for e in range(local):
            scale = jnp.sum(jnp.where(which == ex * local + e, wts, 0.0), axis=1, keepdims=True)
            gate = acc_in[:, 2 * e * hid : (2 * e + 1) * hid]
            up = acc_in[:, (2 * e + 1) * hid : (2 * e + 2) * hid]
            grad = acc_hid[:, e * hid : (e + 1) * hid] * scale
            sig = jax.nn.sigmoid(gate)
            hid_grads[:, 2 * e * hid : (2 * e + 1) * hid] = (
                grad * up * sig * (1.0 + gate * (1.0 - sig))
            ).astype(BF16)
            hid_grads[:, (2 * e + 1) * hid : (2 * e + 2) * hid] = (grad * gate * sig).astype(BF16)
        for half in range(2):
            w_cols = pl.ds(half * half_w, half_w)
            value = jnp.dot(hid_grads[...], w_cat_t[:, w_cols], preferred_element_type=F32)
            value = value.astype(BF16).reshape(2, 2, 2, toks, half_w)
            part[i, half, 0] = value[:, :, 0]
            part[i, half, 1] = value[:, :, 1]
            core_sum[i, half] = send(part.at[i, half, oc], core_got.at[i, half], to_core)

    def add(*refs):
        total = refs[0][...].astype(F32)
        for ref in refs[1:]:
            total = total + ref[...].astype(F32)
        return total.astype(BF16)

    def reduce1(i):
        core_sum[i, 0].wait_recv()
        for by in range(2):
            for bx in range(2):
                sum_a[i, bx, by] = add(part.at[i, 0, c, by, bx], core_got.at[i, 0, by, bx])
        first = send(sum_a.at[i, ox], x_got.at[i], to_x)
        core_sum[i, 1].wait_recv()
        for by in range(2):
            for bx in range(2):
                sum_b[i, by, bx] = add(part.at[i, 1, c, by, bx], core_got.at[i, 1, by, bx])
        stage1[i] = (first, send(sum_b.at[i, oy], y_got.at[i], to_y))

    def reduce2(i):
        stage1[i][0].wait_recv()
        send2[i, 0] = add(sum_a.at[i, x, oy], x_got.at[i, oy])
        first = send(send2.at[i, 0], got2.at[i, 0], to_y)
        stage1[i][1].wait_recv()
        send2[i, 1] = add(sum_b.at[i, y, ox], y_got.at[i, ox])
        stage2[i] = (first, send(send2.at[i, 1], got2.at[i, 1], to_x))

    def reduce3(i):
        stage2[i][0].wait_recv()
        column[i, 0] = add(sum_a.at[i, x, y], x_got.at[i, y], got2.at[i, 0])
        stage2[i][1].wait_recv()
        column[i, 1] = add(sum_b.at[i, y, x], y_got.at[i, x], got2.at[i, 1])
        if i > 0:
            copy = z_copy(column.at[i], z_got.at[z], order[i], z, 1, i)
            copy.start()
            z_sent.append((copy, None))

    turn = 256

    def turn_down(e):
        @pl.loop(0, width // turn)
        def _(j):
            cols = pl.ds(pl.multiple_of(j * turn, turn), turn)
            w_dn_t[cols, e * hid : (e + 1) * hid] = w_dn[e, :, cols].T

    def turn_cat(e):
        span = pl.ds(2 * e * hid, 2 * hid)

        @pl.loop(0, width // turn)
        def _(j):
            cols = pl.ds(pl.multiple_of(j * turn, turn), turn)
            w_cat_t[span, cols] = w_cat[cols, span].T

    to_plane(0)
    for copy in weight_copies:
        copy.wait()
    for e in range(local):
        turn_down(e)
    from_z(1)
    relay(0)
    from_z(2)
    relay(1)
    for e in range(local):
        turn_cat(e)
    share_diagonal(0)
    compute(0)
    from_z(3)
    relay(2)
    share_diagonal(1)
    reduce1(0)
    compute(1)
    relay(3)
    share_diagonal(2)
    reduce1(1)
    reduce2(0)
    compute(2)
    share_diagonal(3)
    reduce1(2)
    reduce2(1)
    reduce3(0)
    compute(3)
    reduce1(3)
    reduce2(2)
    reduce3(1)
    reduce2(3)
    reduce3(2)
    reduce3(3)
    for s in order[1:]:
        got = z_got.at[s]
        z_copy(got, got, s, s, 1, 0).wait_recv()
    for half in range(2):
        out_ref[:, half * half_w : (half + 1) * half_w] = add(
            column.at[0, half], *[z_got.at[s, half] for s in order[1:]]
        )
    for copy in started:
        copy.wait_send()
    for copy, there in z_sent:
        if there is None:
            copy.wait_send()
        else:

            @pl.when(there)
            def _(copy=copy):
                copy.wait_send()


def fused(tokens, out_grad, route_ids, route_probs, w_gate, w_up, w_down):
    toks, width = tokens.shape
    local, _, hid = w_gate.shape
    half_w = width // 2
    rows = 8 * toks
    vmem = pl.BlockSpec(memory_space=pltpu.VMEM)
    hbm = pl.BlockSpec(memory_space=pl.ANY)
    scratch = [
        pltpu.VMEM((4, 2, 2, 2, 2, toks, width + LANES), BF16),
        pltpu.VMEM((width, 2 * local * hid), BF16),
        pltpu.VMEM((local, hid, width), BF16),
        pltpu.VMEM((2 * local * hid, width), BF16),
        pltpu.VMEM((width, local * hid), BF16),
        pltpu.VMEM((rows, 2 * local * hid), F32),
        pltpu.VMEM((rows, local * hid), F32),
        pltpu.VMEM((rows, 2 * local * hid), BF16),
        pltpu.VMEM((4, 2, 2, 2, 2, toks, half_w), BF16),
        pltpu.VMEM((4, 2, 2, 2, toks, half_w), BF16),
        pltpu.VMEM((4, 2, 2, toks, half_w), BF16),
        pltpu.VMEM((4, 2, 2, toks, half_w), BF16),
        pltpu.VMEM((4, 2, toks, half_w), BF16),
        pltpu.VMEM((4, 2, toks, half_w), BF16),
        pltpu.VMEM((4, 2, toks, half_w), BF16),
        pltpu.VMEM((4, 2, toks, half_w), BF16),
        pltpu.VMEM((4, 2, toks, half_w), BF16),
        pltpu.VMEM((4, 2, toks, half_w), BF16),
        pltpu.SemaphoreType.DMA((COPIES,)),
        pltpu.SemaphoreType.DMA((COPIES,)),
        pltpu.SemaphoreType.DMA((2, 5)),
        pltpu.SemaphoreType.DMA((2, 4)),
        pltpu.SemaphoreType.DMA((2 * local + 3,)),
    ]
    flops = 2 * 4 * rows * width * local * hid * 5
    return pl.pallas_call(
        fused_kernel,
        out_shape=jax.ShapeDtypeStruct((toks, width), BF16),
        in_specs=[hbm, hbm, vmem, vmem, hbm, hbm, hbm],
        out_specs=vmem,
        scratch_shapes=scratch,
        compiler_params=pltpu.CompilerParams(
            collective_id=0, has_side_effects=True, vmem_limit_bytes=56 * 1024 * 1024
        ),
        cost_estimate=pl.CostEstimate(
            flops=flops, bytes_accessed=6 * local * hid * width, transcendentals=4 * rows * local * hid
        ),
    )(tokens, out_grad, route_ids.T, route_probs.T, w_gate, w_up, w_down)


def slot_matches(flat_ids, experts, capacity):
    onehot = (flat_ids[:, None] == jnp.arange(experts, dtype=jnp.int32)[None, :]).astype(jnp.int32)
    earlier = jnp.cumsum(onehot, axis=0) - onehot
    slot_rank = jnp.sum(earlier * onehot, axis=1)
    slot_of = flat_ids * capacity + slot_rank
    return slot_of[None, :] == jnp.arange(experts * capacity, dtype=jnp.int32)[:, None]


def select_matrix(matches, tok_count):
    return jnp.sum(matches.reshape(matches.shape[0], tok_count, TOPK).astype(jnp.float32), axis=2)


def build_tiles(token_rows, grad_rows, matches, flat_probs):
    select = select_matrix(matches, token_rows.shape[0]).astype(jnp.bfloat16)
    slot_scale = jnp.sum(jnp.where(matches, flat_probs[None, :], 0.0), axis=1)
    x_rows = jnp.dot(select, token_rows, preferred_element_type=jnp.float32).astype(jnp.bfloat16)
    g_rows = (
        jnp.dot(select, grad_rows, preferred_element_type=jnp.float32) * slot_scale[:, None]
    ).astype(jnp.bfloat16)
    return jnp.stack([x_rows, g_rows])


def expert_grads(tiles, w_gate, w_up, w_down):
    x_rows = tiles[:, 0]
    g_rows = tiles[:, 1]
    gate_pre = jnp.einsum("nsecd,edh->nsech", x_rows, w_gate, preferred_element_type=jnp.float32)
    up_pre = jnp.einsum("nsecd,edh->nsech", x_rows, w_up, preferred_element_type=jnp.float32)
    hidden_grad = jnp.einsum("nsecd,ehd->nsech", g_rows, w_down, preferred_element_type=jnp.float32)
    sigmoid_a = jax.nn.sigmoid(gate_pre)
    gate_grad = (hidden_grad * up_pre * sigmoid_a * (1.0 + gate_pre * (1.0 - sigmoid_a))).astype(
        jnp.bfloat16
    )
    up_grad = (hidden_grad * gate_pre * sigmoid_a).astype(jnp.bfloat16)
    partial_value = jnp.einsum(
        "nsech,edh->nsecd", gate_grad, w_gate, preferred_element_type=jnp.float32
    )
    partial_value = partial_value + jnp.einsum(
        "nsech,edh->nsecd", up_grad, w_up, preferred_element_type=jnp.float32
    )
    return partial_value.astype(jnp.bfloat16)


def on_device(tokens, out_grad, route_ids, route_probs, w_gate, w_up, w_down):
    columns = lax.axis_size("expert")
    local_experts = w_gate.shape[0]
    experts = local_experts * columns
    tok_count, width = tokens.shape
    capacity = max(2, 2 * tok_count * TOPK // experts)
    slots = experts * capacity
    tile_shape = (2, columns, local_experts, capacity, width)
    own_matches = slot_matches(route_ids.reshape(-1), experts, capacity)
    tiles = build_tiles(tokens, out_grad, own_matches, route_probs.reshape(-1)).reshape(
        (1,) + tile_shape
    )
    received = lax.all_to_all(tiles, "expert", split_axis=2, concat_axis=2, tiled=True)
    partials = expert_grads(
        lax.all_gather(received, "dp", axis=0, tiled=True), w_gate, w_up, w_down
    )
    summed = lax.psum_scatter(
        partials.astype(jnp.float32).astype(jnp.bfloat16), "dp", scatter_dimension=0, tiled=True
    ).astype(jnp.float32)
    returned = lax.all_to_all(
        summed.astype(jnp.bfloat16), "expert", split_axis=1, concat_axis=1, tiled=True
    ).astype(summed.dtype)
    own_select = select_matrix(own_matches, tok_count)
    result = jnp.dot(own_select.T, returned.reshape(slots, width), precision=lax.Precision.HIGHEST)
    return result.astype(jnp.bfloat16)


def solution(mesh):
    placed = (
        P(("dp", "expert"), None),
        P(("dp", "expert"), None),
        P(("dp", "expert"), None),
        P(("dp", "expert"), None),
        P("expert", None, "dp"),
        P("expert", None, "dp"),
        P("expert", "dp", None),
    )
    whole_block = dict(mesh.shape) == {"dp": 4, "expert": 8}

    def chosen(tokens, out_grad, route_ids, route_probs, w_gate, w_up, w_down):
        experts = w_gate.shape[0] * mesh.shape["expert"]
        dense = 2 * tokens.shape[0] * TOPK // experts >= tokens.shape[0]
        fits = tokens.shape[0] == 16 and experts <= LANES
        step = fused if whole_block and dense and fits else on_device
        return step(tokens, out_grad, route_ids, route_probs, w_gate, w_up, w_down)

    return jax.shard_map(
        chosen, mesh=mesh, in_specs=placed, out_specs=P(("dp", "expert"), None), check_vma=False
    )
```

```python
import jax
import jax.numpy as jnp
from jax import lax
from jax.experimental import pallas as pl
from jax.experimental.pallas import tpu as pltpu
from jax.sharding import PartitionSpec as P

TOPK = 8
LANES = 128
MESH = pl.DeviceIdType.MESH
BF16 = jnp.bfloat16
F32 = jnp.float32
COPIES = 80
NT = (((1,), (1,)), ((), ()))


def fused_kernel(
    tokens_ref, grads_ref, ids_ref, probs_ref, w_gate_ref, w_up_ref, w_down_ref, out_ref,
    rows_buf, w_cat, w_dn, w_cat_t, w_dn_t, acc_in, acc_hid, hid_grads, part, core_got, sum_a, sum_b,
    x_got, y_got, send2, got2, column, z_got, send_sems, recv_sems, z_send_sems, z_recv_sems, local_sems,
):
    dp, ex = lax.axis_index("dp"), lax.axis_index("expert")
    y, x = dp // 2, dp % 2
    z, c = ex // 2, ex % 2
    oy, ox, oc = 1 - y, 1 - x, 1 - c
    to_x, to_y, to_core = (y * 2 + ox, ex), (oy * 2 + x, ex), (dp, z * 2 + oc)
    to_z = {k: (dp, ((z + k) % 4) * 2 + c) for k in (1, 2, 3)}
    toks, width = tokens_ref.shape
    half_w = width // 2
    local, _, hid = w_gate_ref.shape
    started = []

    def send(src, dst, device):
        at = len(started)
        copy = pltpu.make_async_remote_copy(
            src_ref=src, dst_ref=dst, send_sem=send_sems.at[at], recv_sem=recv_sems.at[at],
            device_id=device, device_id_type=MESH,
        )
        copy.start()
        started.append(copy)
        return copy

    barrier = pltpu.get_barrier_semaphore()
    for device in (to_x, to_y, to_core, to_z[1], to_z[2], to_z[3]):
        pl.semaphore_signal(barrier, inc=1, device_id=device, device_id_type=MESH)

    own = rows_buf.at[z, y, x, c]
    row_copies = [
        pltpu.make_async_copy(ref, own.at[n, :, pl.ds(0, width)], local_sems.at[n])
        for n, ref in enumerate((tokens_ref, grads_ref))
    ]
    weight_copies = []
    for e in range(local):
        for n, ref in enumerate((w_gate_ref, w_up_ref)):
            weight_copies.append(
                pltpu.make_async_copy(
                    ref.at[e],
                    w_cat.at[:, pl.ds((2 * e + n) * hid, hid)],
                    local_sems.at[2 + 2 * e + n],
                )
            )
    weight_copies.insert(0, pltpu.make_async_copy(w_down_ref, w_dn, local_sems.at[2 + 2 * local]))
    for copy in row_copies + weight_copies:
        copy.start()

    expert = lax.broadcasted_iota(jnp.int32, (LANES, toks), 0)
    weights = jnp.zeros(expert.shape, F32)
    for k in range(TOPK):
        weights = weights + jnp.where(ids_ref[k : k + 1, :] == expert, probs_ref[k : k + 1, :], 0.0)
    high = weights.astype(BF16)
    low = (weights - high.astype(F32)).astype(BF16)
    diagonal = lax.broadcasted_iota(jnp.int32, (toks, toks), 0) == lax.broadcasted_iota(
        jnp.int32, (toks, toks), 1
    )
    eye = jnp.where(diagonal, 1.0, 0.0).astype(BF16)
    for copy in row_copies:
        copy.wait()
    for n, value in enumerate((high, low)):
        turned = lax.dot_general(eye, value, NT, preferred_element_type=F32)
        rows_buf[z, y, x, c, n, :, width:] = turned.astype(BF16)

    pl.semaphore_wait(barrier, 6)

    upper = z // 2
    inner = z + upper * (3 - 2 * z)
    order = [z] + [f + upper * (3 - 2 * f) for f in (1 - inner, 2, 3)]
    x_in, y_in, diag_in = {}, {}, {}
    z_sent = []
    core_in = {i: [] for i in range(4)}
    core_sum, stage1, stage2 = {}, {}, {}

    def z_copy(src, dst, target, source, kind, at):
        return pltpu.make_async_remote_copy(
            src_ref=src, dst_ref=dst, send_sem=z_send_sems.at[kind, at],
            recv_sem=z_recv_sems.at[kind, source],
            device_id=(dp, target * 2 + c), device_id_type=MESH,
        )

    def along_z(source, target, at):
        got = rows_buf.at[source, y, x, c]
        copy = z_copy(got, got, target, source, 0, at)
        there = jnp.logical_and(target >= 0, target <= 3)

        @pl.when(there)
        def _():
            copy.start()

        z_sent.append((copy, there))

    def to_plane(i):
        got = rows_buf.at[order[i], y, x, c]
        x_in[i] = send(got, got, to_x)
        y_in[i] = send(got, got, to_y)
        if i == 0:
            along_z(z, z - 1, 0)
            along_z(z, z + 1, 4)
        core_in[i].append(send(got, got, to_core))

    def from_z(i):
        s = order[i]
        got = rows_buf.at[s, y, x, c]
        z_copy(got, got, s, s, 0, 0).wait_recv()
        up = (z + 4 - s) // 4
        along_z(s, z + 2 * up - 1, i)
        to_plane(i)

    def relay(i, parts=("core", "diagonal")):
        got_x = rows_buf.at[order[i], y, ox, c]
        got_y = rows_buf.at[order[i], oy, x, c]
        if parts[0] == "core":
            x_in[i].wait_recv()
        if "diagonal" in parts:
            first = send(got_x.at[0], got_x.at[0], to_y)
        if parts[0] == "core":
            core_in[i].append(send(got_x, got_x, to_core))
            y_in[i].wait_recv()
        if "diagonal" in parts:
            diag_in[i] = (first, send(got_y.at[1], got_y.at[1], to_x))
        if parts[0] == "core":
            core_in[i].append(send(got_y, got_y, to_core))

    def share_diagonal(i):
        for n in range(2):
            diag_in[i][n].wait_recv()
            got = rows_buf.at[order[i], oy, ox, c, n]
            core_in[i].append(send(got, got, to_core))

    rows = 8 * toks
    k_tile = width // 2

    def compute(i, between):
        for copy in core_in[i]:
            copy.wait_recv()
        s = order[i]
        acc_in[...] = jnp.zeros_like(acc_in)
        acc_hid[...] = jnp.zeros_like(acc_hid)

        @pl.loop(0, width // k_tile)
        def _(k):
            cols = pl.ds(pl.multiple_of(k * k_tile, LANES), k_tile)
            x_rows = rows_buf[s, :, :, :, 0, :, cols].reshape(rows, k_tile)
            g_rows = rows_buf[s, :, :, :, 1, :, cols].reshape(rows, k_tile)
            acc_in[...] += jnp.dot(x_rows, w_cat[cols, :], preferred_element_type=F32)
            acc_hid[...] += jnp.dot(g_rows, w_dn_t[cols, :], preferred_element_type=F32)

        tail = pl.ds(width, LANES)
        wts = rows_buf[s, :, :, :, 0, :, tail].reshape(rows, LANES).astype(F32)
        wts = wts + rows_buf[s, :, :, :, 1, :, tail].reshape(rows, LANES).astype(F32)
        which = lax.broadcasted_iota(jnp.int32, (rows, LANES), 1)
        for e in range(local):
            scale = jnp.sum(jnp.where(which == ex * local + e, wts, 0.0), axis=1, keepdims=True)
            gate = acc_in[:, 2 * e * hid : (2 * e + 1) * hid]
            up = acc_in[:, (2 * e + 1) * hid : (2 * e + 2) * hid]
            grad = acc_hid[:, e * hid : (e + 1) * hid] * scale
            sig = jax.nn.sigmoid(gate)
            hid_grads[:, 2 * e * hid : (2 * e + 1) * hid] = (
                grad * up * sig * (1.0 + gate * (1.0 - sig))
            ).astype(BF16)
            hid_grads[:, (2 * e + 1) * hid : (2 * e + 2) * hid] = (grad * gate * sig).astype(BF16)
        between()
        for half in range(2):
            w_cols = pl.ds(half * half_w, half_w)
            value = jnp.dot(hid_grads[...], w_cat_t[:, w_cols], preferred_element_type=F32)
            value = value.astype(BF16).reshape(2, 2, 2, toks, half_w)
            part[i, half, 0] = value[:, :, 0]
            part[i, half, 1] = value[:, :, 1]
            core_sum[i, half] = send(part.at[i, half, oc], core_got.at[i, half], to_core)

    def add(*refs):
        total = refs[0][...].astype(F32)
        for ref in refs[1:]:
            total = total + ref[...].astype(F32)
        return total.astype(BF16)

    def reduce1(i):
        core_sum[i, 0].wait_recv()
        for by in range(2):
            for bx in range(2):
                sum_a[i, bx, by] = add(part.at[i, 0, c, by, bx], core_got.at[i, 0, by, bx])
        first = send(sum_a.at[i, ox], x_got.at[i], to_x)
        core_sum[i, 1].wait_recv()
        for by in range(2):
            for bx in range(2):
                sum_b[i, by, bx] = add(part.at[i, 1, c, by, bx], core_got.at[i, 1, by, bx])
        stage1[i] = (first, send(sum_b.at[i, oy], y_got.at[i], to_y))

    def reduce2(i):
        stage1[i][0].wait_recv()
        send2[i, 0] = add(sum_a.at[i, x, oy], x_got.at[i, oy])
        first = send(send2.at[i, 0], got2.at[i, 0], to_y)
        stage1[i][1].wait_recv()
        send2[i, 1] = add(sum_b.at[i, y, ox], y_got.at[i, ox])
        stage2[i] = (first, send(send2.at[i, 1], got2.at[i, 1], to_x))

    def reduce3(i):
        stage2[i][0].wait_recv()
        column[i, 0] = add(sum_a.at[i, x, y], x_got.at[i, y], got2.at[i, 0])
        stage2[i][1].wait_recv()
        column[i, 1] = add(sum_b.at[i, y, x], y_got.at[i, x], got2.at[i, 1])
        if i > 0:
            copy = z_copy(column.at[i], z_got.at[z], order[i], z, 1, i)
            copy.start()
            z_sent.append((copy, None))

    turn = 256

    def turn_down(e):
        @pl.loop(0, width // turn)
        def _(j):
            cols = pl.ds(pl.multiple_of(j * turn, turn), turn)
            w_dn_t[cols, e * hid : (e + 1) * hid] = w_dn[e, :, cols].T

    def turn_cat(e):
        span = pl.ds(2 * e * hid, 2 * hid)

        @pl.loop(0, width // turn)
        def _(j):
            cols = pl.ds(pl.multiple_of(j * turn, turn), turn)
            w_cat_t[span, cols] = w_cat[cols, span].T

    to_plane(0)
    for copy in weight_copies:
        copy.wait()
    for e in range(local):
        turn_down(e)
    from_z(1)
    relay(0, ("core",))
    from_z(2)
    relay(1)
    for e in range(local):
        turn_cat(e)
    share_diagonal(1)
    compute(1, lambda: from_z(3))
    relay(2)
    reduce1(1)
    share_diagonal(2)
    compute(2, lambda: reduce2(1))
    relay(3)
    relay(0, ("diagonal",))
    reduce1(2)
    reduce3(1)
    share_diagonal(3)
    compute(3, lambda: reduce2(2))
    share_diagonal(0)
    reduce1(3)
    reduce3(2)
    compute(0, lambda: reduce2(3))
    reduce3(3)
    reduce1(0)
    reduce2(0)
    reduce3(0)
    for s in order[1:]:
        got = z_got.at[s]
        z_copy(got, got, s, s, 1, 0).wait_recv()
    for half in range(2):
        out_ref[:, half * half_w : (half + 1) * half_w] = add(
            column.at[0, half], *[z_got.at[s, half] for s in order[1:]]
        )
    for copy in started:
        copy.wait_send()
    for copy, there in z_sent:
        if there is None:
            copy.wait_send()
        else:

            @pl.when(there)
            def _(copy=copy):
                copy.wait_send()


def fused(tokens, out_grad, route_ids, route_probs, w_gate, w_up, w_down):
    toks, width = tokens.shape
    local, _, hid = w_gate.shape
    half_w = width // 2
    rows = 8 * toks
    vmem = pl.BlockSpec(memory_space=pltpu.VMEM)
    hbm = pl.BlockSpec(memory_space=pl.ANY)
    scratch = [
        pltpu.VMEM((4, 2, 2, 2, 2, toks, width + LANES), BF16),
        pltpu.VMEM((width, 2 * local * hid), BF16),
        pltpu.VMEM((local, hid, width), BF16),
        pltpu.VMEM((2 * local * hid, width), BF16),
        pltpu.VMEM((width, local * hid), BF16),
        pltpu.VMEM((rows, 2 * local * hid), F32),
        pltpu.VMEM((rows, local * hid), F32),
        pltpu.VMEM((rows, 2 * local * hid), BF16),
        pltpu.VMEM((4, 2, 2, 2, 2, toks, half_w), BF16),
        pltpu.VMEM((4, 2, 2, 2, toks, half_w), BF16),
        pltpu.VMEM((4, 2, 2, toks, half_w), BF16),
        pltpu.VMEM((4, 2, 2, toks, half_w), BF16),
        pltpu.VMEM((4, 2, toks, half_w), BF16),
        pltpu.VMEM((4, 2, toks, half_w), BF16),
        pltpu.VMEM((4, 2, toks, half_w), BF16),
        pltpu.VMEM((4, 2, toks, half_w), BF16),
        pltpu.VMEM((4, 2, toks, half_w), BF16),
        pltpu.VMEM((4, 2, toks, half_w), BF16),
        pltpu.SemaphoreType.DMA((COPIES,)),
        pltpu.SemaphoreType.DMA((COPIES,)),
        pltpu.SemaphoreType.DMA((2, 5)),
        pltpu.SemaphoreType.DMA((2, 4)),
        pltpu.SemaphoreType.DMA((2 * local + 3,)),
    ]
    flops = 2 * 4 * rows * width * local * hid * 5
    return pl.pallas_call(
        fused_kernel,
        out_shape=jax.ShapeDtypeStruct((toks, width), BF16),
        in_specs=[hbm, hbm, vmem, vmem, hbm, hbm, hbm],
        out_specs=vmem,
        scratch_shapes=scratch,
        compiler_params=pltpu.CompilerParams(
            collective_id=0, has_side_effects=True, vmem_limit_bytes=56 * 1024 * 1024
        ),
        cost_estimate=pl.CostEstimate(
            flops=flops, bytes_accessed=6 * local * hid * width, transcendentals=4 * rows * local * hid
        ),
    )(tokens, out_grad, route_ids.T, route_probs.T, w_gate, w_up, w_down)


def slot_matches(flat_ids, experts, capacity):
    onehot = (flat_ids[:, None] == jnp.arange(experts, dtype=jnp.int32)[None, :]).astype(jnp.int32)
    earlier = jnp.cumsum(onehot, axis=0) - onehot
    slot_rank = jnp.sum(earlier * onehot, axis=1)
    slot_of = flat_ids * capacity + slot_rank
    return slot_of[None, :] == jnp.arange(experts * capacity, dtype=jnp.int32)[:, None]


def select_matrix(matches, tok_count):
    return jnp.sum(matches.reshape(matches.shape[0], tok_count, TOPK).astype(jnp.float32), axis=2)


def build_tiles(token_rows, grad_rows, matches, flat_probs):
    select = select_matrix(matches, token_rows.shape[0]).astype(jnp.bfloat16)
    slot_scale = jnp.sum(jnp.where(matches, flat_probs[None, :], 0.0), axis=1)
    x_rows = jnp.dot(select, token_rows, preferred_element_type=jnp.float32).astype(jnp.bfloat16)
    g_rows = (
        jnp.dot(select, grad_rows, preferred_element_type=jnp.float32) * slot_scale[:, None]
    ).astype(jnp.bfloat16)
    return jnp.stack([x_rows, g_rows])


def expert_grads(tiles, w_gate, w_up, w_down):
    x_rows = tiles[:, 0]
    g_rows = tiles[:, 1]
    gate_pre = jnp.einsum("nsecd,edh->nsech", x_rows, w_gate, preferred_element_type=jnp.float32)
    up_pre = jnp.einsum("nsecd,edh->nsech", x_rows, w_up, preferred_element_type=jnp.float32)
    hidden_grad = jnp.einsum("nsecd,ehd->nsech", g_rows, w_down, preferred_element_type=jnp.float32)
    sigmoid_a = jax.nn.sigmoid(gate_pre)
    gate_grad = (hidden_grad * up_pre * sigmoid_a * (1.0 + gate_pre * (1.0 - sigmoid_a))).astype(
        jnp.bfloat16
    )
    up_grad = (hidden_grad * gate_pre * sigmoid_a).astype(jnp.bfloat16)
    partial_value = jnp.einsum(
        "nsech,edh->nsecd", gate_grad, w_gate, preferred_element_type=jnp.float32
    )
    partial_value = partial_value + jnp.einsum(
        "nsech,edh->nsecd", up_grad, w_up, preferred_element_type=jnp.float32
    )
    return partial_value.astype(jnp.bfloat16)


def on_device(tokens, out_grad, route_ids, route_probs, w_gate, w_up, w_down):
    columns = lax.axis_size("expert")
    local_experts = w_gate.shape[0]
    experts = local_experts * columns
    tok_count, width = tokens.shape
    capacity = max(2, 2 * tok_count * TOPK // experts)
    slots = experts * capacity
    tile_shape = (2, columns, local_experts, capacity, width)
    own_matches = slot_matches(route_ids.reshape(-1), experts, capacity)
    tiles = build_tiles(tokens, out_grad, own_matches, route_probs.reshape(-1)).reshape(
        (1,) + tile_shape
    )
    received = lax.all_to_all(tiles, "expert", split_axis=2, concat_axis=2, tiled=True)
    partials = expert_grads(
        lax.all_gather(received, "dp", axis=0, tiled=True), w_gate, w_up, w_down
    )
    summed = lax.psum_scatter(
        partials.astype(jnp.float32).astype(jnp.bfloat16), "dp", scatter_dimension=0, tiled=True
    ).astype(jnp.float32)
    returned = lax.all_to_all(
        summed.astype(jnp.bfloat16), "expert", split_axis=1, concat_axis=1, tiled=True
    ).astype(summed.dtype)
    own_select = select_matrix(own_matches, tok_count)
    result = jnp.dot(own_select.T, returned.reshape(slots, width), precision=lax.Precision.HIGHEST)
    return result.astype(jnp.bfloat16)


def solution(mesh):
    placed = (
        P(("dp", "expert"), None),
        P(("dp", "expert"), None),
        P(("dp", "expert"), None),
        P(("dp", "expert"), None),
        P("expert", None, "dp"),
        P("expert", None, "dp"),
        P("expert", "dp", None),
    )
    whole_block = dict(mesh.shape) == {"dp": 4, "expert": 8}

    def chosen(tokens, out_grad, route_ids, route_probs, w_gate, w_up, w_down):
        experts = w_gate.shape[0] * mesh.shape["expert"]
        dense = 2 * tokens.shape[0] * TOPK // experts >= tokens.shape[0]
        fits = tokens.shape[0] == 16 and experts <= LANES
        step = fused if whole_block and dense and fits else on_device
        return step(tokens, out_grad, route_ids, route_probs, w_gate, w_up, w_down)

    return jax.shard_map(
        chosen, mesh=mesh, in_specs=placed, out_specs=P(("dp", "expert"), None), check_vma=False
    )
```

```python
import jax
import jax.numpy as jnp
from jax import lax
from jax.experimental import pallas as pl
from jax.experimental.pallas import tpu as pltpu
from jax.sharding import PartitionSpec as P

TOPK = 8
LANES = 128
MESH = pl.DeviceIdType.MESH
BF16 = jnp.bfloat16
F32 = jnp.float32
COPIES = 80
NT = (((1,), (1,)), ((), ()))


def fused_kernel(
    tokens_ref, grads_ref, ids_ref, probs_ref, w_gate_ref, w_up_ref, w_down_ref, out_ref,
    rows_buf, w_cat, w_dn, w_cat_t, w_dn_t, acc_in, acc_hid, hid_grads, part, core_got, sum_a, sum_b,
    x_got, y_got, send2, got2, column, z_got, send_sems, recv_sems, z_send_sems, z_recv_sems, local_sems,
):
    dp, ex = lax.axis_index("dp"), lax.axis_index("expert")
    y, x = dp // 2, dp % 2
    z, c = ex // 2, ex % 2
    oy, ox, oc = 1 - y, 1 - x, 1 - c
    to_x, to_y, to_core = (y * 2 + ox, ex), (oy * 2 + x, ex), (dp, z * 2 + oc)
    to_z = {k: (dp, ((z + k) % 4) * 2 + c) for k in (1, 2, 3)}
    toks, width = tokens_ref.shape
    half_w = width // 2
    local, _, hid = w_gate_ref.shape
    started = []

    def send(src, dst, device):
        at = len(started)
        copy = pltpu.make_async_remote_copy(
            src_ref=src, dst_ref=dst, send_sem=send_sems.at[at], recv_sem=recv_sems.at[at],
            device_id=device, device_id_type=MESH,
        )
        copy.start()
        started.append(copy)
        return copy

    barrier = pltpu.get_barrier_semaphore()
    for device in (to_x, to_y, to_core, to_z[1], to_z[2], to_z[3]):
        pl.semaphore_signal(barrier, inc=1, device_id=device, device_id_type=MESH)

    own = rows_buf.at[z, y, x, c]
    row_copies = [
        pltpu.make_async_copy(ref, own.at[n, :, pl.ds(0, width)], local_sems.at[n])
        for n, ref in enumerate((tokens_ref, grads_ref))
    ]
    weight_copies = []
    for e in range(local):
        for n, ref in enumerate((w_gate_ref, w_up_ref)):
            weight_copies.append(
                pltpu.make_async_copy(
                    ref.at[e],
                    w_cat.at[:, pl.ds((2 * e + n) * hid, hid)],
                    local_sems.at[2 + 2 * e + n],
                )
            )
    weight_copies.insert(0, pltpu.make_async_copy(w_down_ref, w_dn, local_sems.at[2 + 2 * local]))
    for copy in row_copies + weight_copies:
        copy.start()

    expert = lax.broadcasted_iota(jnp.int32, (LANES, toks), 0)
    weights = jnp.zeros(expert.shape, F32)
    for k in range(TOPK):
        weights = weights + jnp.where(ids_ref[k : k + 1, :] == expert, probs_ref[k : k + 1, :], 0.0)
    high = weights.astype(BF16)
    low = (weights - high.astype(F32)).astype(BF16)
    diagonal = lax.broadcasted_iota(jnp.int32, (toks, toks), 0) == lax.broadcasted_iota(
        jnp.int32, (toks, toks), 1
    )
    eye = jnp.where(diagonal, 1.0, 0.0).astype(BF16)
    for copy in row_copies:
        copy.wait()
    for n, value in enumerate((high, low)):
        turned = lax.dot_general(eye, value, NT, preferred_element_type=F32)
        rows_buf[z, y, x, c, n, :, width:] = turned.astype(BF16)

    pl.semaphore_wait(barrier, 6)

    upper = z // 2
    inner = z + upper * (3 - 2 * z)
    order = [z] + [f + upper * (3 - 2 * f) for f in (1 - inner, 2, 3)]
    x_in, y_in, diag_in = {}, {}, {}
    z_sent = []
    core_in = {i: [] for i in range(4)}
    core_sum, stage1, stage2 = {}, {}, {}

    def z_copy(src, dst, target, source, kind, at):
        return pltpu.make_async_remote_copy(
            src_ref=src, dst_ref=dst, send_sem=z_send_sems.at[kind, at],
            recv_sem=z_recv_sems.at[kind, source],
            device_id=(dp, target * 2 + c), device_id_type=MESH,
        )

    def along_z(source, target, at):
        got = rows_buf.at[source, y, x, c]
        copy = z_copy(got, got, target, source, 0, at)
        there = jnp.logical_and(target >= 0, target <= 3)

        @pl.when(there)
        def _():
            copy.start()

        z_sent.append((copy, there))

    def to_plane(i):
        got = rows_buf.at[order[i], y, x, c]
        x_in[i] = send(got, got, to_x)
        y_in[i] = send(got, got, to_y)
        if i == 0:
            along_z(z, z - 1, 0)
            along_z(z, z + 1, 4)
        core_in[i].append(send(got, got, to_core))

    def from_z(i):
        s = order[i]
        got = rows_buf.at[s, y, x, c]
        z_copy(got, got, s, s, 0, 0).wait_recv()
        up = (z + 4 - s) // 4
        along_z(s, z + 2 * up - 1, i)
        to_plane(i)

    def relay(i):
        x_in[i].wait_recv()
        got = rows_buf.at[order[i], y, ox, c]
        first = send(got.at[0], got.at[0], to_y)
        core_in[i].append(send(got, got, to_core))
        y_in[i].wait_recv()
        got = rows_buf.at[order[i], oy, x, c]
        diag_in[i] = (first, send(got.at[1], got.at[1], to_x))
        core_in[i].append(send(got, got, to_core))

    def share_diagonal(i):
        for n in range(2):
            diag_in[i][n].wait_recv()
            got = rows_buf.at[order[i], oy, ox, c, n]
            core_in[i].append(send(got, got, to_core))

    rows = 8 * toks
    k_tile = width // 2

    def compute(i, between=lambda: None):
        for copy in core_in[i]:
            copy.wait_recv()
        s = order[i]
        acc_in[...] = jnp.zeros_like(acc_in)
        acc_hid[...] = jnp.zeros_like(acc_hid)

        @pl.loop(0, width // k_tile)
        def _(k):
            cols = pl.ds(pl.multiple_of(k * k_tile, LANES), k_tile)
            x_rows = rows_buf[s, :, :, :, 0, :, cols].reshape(rows, k_tile)
            g_rows = rows_buf[s, :, :, :, 1, :, cols].reshape(rows, k_tile)
            acc_in[...] += jnp.dot(x_rows, w_cat[cols, :], preferred_element_type=F32)
            acc_hid[...] += jnp.dot(g_rows, w_dn_t[cols, :], preferred_element_type=F32)

        tail = pl.ds(width, LANES)
        wts = rows_buf[s, :, :, :, 0, :, tail].reshape(rows, LANES).astype(F32)
        wts = wts + rows_buf[s, :, :, :, 1, :, tail].reshape(rows, LANES).astype(F32)
        which = lax.broadcasted_iota(jnp.int32, (rows, LANES), 1)
        for e in range(local):
            scale = jnp.sum(jnp.where(which == ex * local + e, wts, 0.0), axis=1, keepdims=True)
            gate = acc_in[:, 2 * e * hid : (2 * e + 1) * hid]
            up = acc_in[:, (2 * e + 1) * hid : (2 * e + 2) * hid]
            grad = acc_hid[:, e * hid : (e + 1) * hid] * scale
            sig = jax.nn.sigmoid(gate)
            hid_grads[:, 2 * e * hid : (2 * e + 1) * hid] = (
                grad * up * sig * (1.0 + gate * (1.0 - sig))
            ).astype(BF16)
            hid_grads[:, (2 * e + 1) * hid : (2 * e + 2) * hid] = (grad * gate * sig).astype(BF16)
        between()
        for half in range(2):
            w_cols = pl.ds(half * half_w, half_w)
            value = jnp.dot(hid_grads[...], w_cat_t[:, w_cols], preferred_element_type=F32)
            value = value.astype(BF16).reshape(2, 2, 2, toks, half_w)
            part[i, half, 0] = value[:, :, 0]
            part[i, half, 1] = value[:, :, 1]
            core_sum[i, half] = send(part.at[i, half, oc], core_got.at[i, half], to_core)

    def add(*refs):
        total = refs[0][...].astype(F32)
        for ref in refs[1:]:
            total = total + ref[...].astype(F32)
        return total.astype(BF16)

    def reduce1(i):
        core_sum[i, 0].wait_recv()
        for by in range(2):
            for bx in range(2):
                sum_a[i, bx, by] = add(part.at[i, 0, c, by, bx], core_got.at[i, 0, by, bx])
        first = send(sum_a.at[i, ox], x_got.at[i], to_x)
        core_sum[i, 1].wait_recv()
        for by in range(2):
            for bx in range(2):
                sum_b[i, by, bx] = add(part.at[i, 1, c, by, bx], core_got.at[i, 1, by, bx])
        stage1[i] = (first, send(sum_b.at[i, oy], y_got.at[i], to_y))

    def reduce2(i):
        stage1[i][0].wait_recv()
        send2[i, 0] = add(sum_a.at[i, x, oy], x_got.at[i, oy])
        first = send(send2.at[i, 0], got2.at[i, 0], to_y)
        stage1[i][1].wait_recv()
        send2[i, 1] = add(sum_b.at[i, y, ox], y_got.at[i, ox])
        stage2[i] = (first, send(send2.at[i, 1], got2.at[i, 1], to_x))

    def reduce3(i):
        stage2[i][0].wait_recv()
        column[i, 0] = add(sum_a.at[i, x, y], x_got.at[i, y], got2.at[i, 0])
        stage2[i][1].wait_recv()
        column[i, 1] = add(sum_b.at[i, y, x], y_got.at[i, x], got2.at[i, 1])
        if i > 0:
            copy = z_copy(column.at[i], z_got.at[z], order[i], z, 1, i)
            copy.start()
            z_sent.append((copy, None))

    turn = 256

    def turn_down(e):
        @pl.loop(0, width // turn)
        def _(j):
            cols = pl.ds(pl.multiple_of(j * turn, turn), turn)
            w_dn_t[cols, e * hid : (e + 1) * hid] = w_dn[e, :, cols].T

    def turn_cat(e):
        span = pl.ds(2 * e * hid, 2 * hid)

        @pl.loop(0, width // turn)
        def _(j):
            cols = pl.ds(pl.multiple_of(j * turn, turn), turn)
            w_cat_t[span, cols] = w_cat[cols, span].T

    to_plane(0)
    weight_copies[0].wait()
    for e in range(local):
        turn_down(e)
    from_z(1)
    relay(0)
    for copy in weight_copies[1:]:
        copy.wait()
    for e in range(local):
        turn_cat(e)
    from_z(2)
    share_diagonal(0)
    compute(0, lambda: relay(1))
    from_z(3)
    reduce1(0)
    relay(2)
    share_diagonal(1)
    compute(1)
    relay(3)
    reduce1(1)
    reduce2(0)
    share_diagonal(2)
    compute(2)
    share_diagonal(3)
    reduce1(2)
    reduce2(1)
    reduce3(0)
    compute(3, lambda: reduce2(2))
    reduce3(1)
    reduce1(3)
    reduce3(2)
    reduce2(3)
    reduce3(3)
    for s in order[1:]:
        got = z_got.at[s]
        z_copy(got, got, s, s, 1, 0).wait_recv()
    for half in range(2):
        out_ref[:, half * half_w : (half + 1) * half_w] = add(
            column.at[0, half], *[z_got.at[s, half] for s in order[1:]]
        )
    for copy in started:
        copy.wait_send()
    for copy, there in z_sent:
        if there is None:
            copy.wait_send()
        else:

            @pl.when(there)
            def _(copy=copy):
                copy.wait_send()


def fused(tokens, out_grad, route_ids, route_probs, w_gate, w_up, w_down):
    toks, width = tokens.shape
    local, _, hid = w_gate.shape
    half_w = width // 2
    rows = 8 * toks
    vmem = pl.BlockSpec(memory_space=pltpu.VMEM)
    hbm = pl.BlockSpec(memory_space=pl.ANY)
    scratch = [
        pltpu.VMEM((4, 2, 2, 2, 2, toks, width + LANES), BF16),
        pltpu.VMEM((width, 2 * local * hid), BF16),
        pltpu.VMEM((local, hid, width), BF16),
        pltpu.VMEM((2 * local * hid, width), BF16),
        pltpu.VMEM((width, local * hid), BF16),
        pltpu.VMEM((rows, 2 * local * hid), F32),
        pltpu.VMEM((rows, local * hid), F32),
        pltpu.VMEM((rows, 2 * local * hid), BF16),
        pltpu.VMEM((4, 2, 2, 2, 2, toks, half_w), BF16),
        pltpu.VMEM((4, 2, 2, 2, toks, half_w), BF16),
        pltpu.VMEM((4, 2, 2, toks, half_w), BF16),
        pltpu.VMEM((4, 2, 2, toks, half_w), BF16),
        pltpu.VMEM((4, 2, toks, half_w), BF16),
        pltpu.VMEM((4, 2, toks, half_w), BF16),
        pltpu.VMEM((4, 2, toks, half_w), BF16),
        pltpu.VMEM((4, 2, toks, half_w), BF16),
        pltpu.VMEM((4, 2, toks, half_w), BF16),
        pltpu.VMEM((4, 2, toks, half_w), BF16),
        pltpu.SemaphoreType.DMA((COPIES,)),
        pltpu.SemaphoreType.DMA((COPIES,)),
        pltpu.SemaphoreType.DMA((2, 5)),
        pltpu.SemaphoreType.DMA((2, 4)),
        pltpu.SemaphoreType.DMA((2 * local + 3,)),
    ]
    flops = 2 * 4 * rows * width * local * hid * 5
    return pl.pallas_call(
        fused_kernel,
        out_shape=jax.ShapeDtypeStruct((toks, width), BF16),
        in_specs=[hbm, hbm, vmem, vmem, hbm, hbm, hbm],
        out_specs=vmem,
        scratch_shapes=scratch,
        compiler_params=pltpu.CompilerParams(
            collective_id=0, has_side_effects=True, vmem_limit_bytes=56 * 1024 * 1024
        ),
        cost_estimate=pl.CostEstimate(
            flops=flops, bytes_accessed=6 * local * hid * width, transcendentals=4 * rows * local * hid
        ),
    )(tokens, out_grad, route_ids.T, route_probs.T, w_gate, w_up, w_down)


def slot_matches(flat_ids, experts, capacity):
    onehot = (flat_ids[:, None] == jnp.arange(experts, dtype=jnp.int32)[None, :]).astype(jnp.int32)
    earlier = jnp.cumsum(onehot, axis=0) - onehot
    slot_rank = jnp.sum(earlier * onehot, axis=1)
    slot_of = flat_ids * capacity + slot_rank
    return slot_of[None, :] == jnp.arange(experts * capacity, dtype=jnp.int32)[:, None]


def select_matrix(matches, tok_count):
    return jnp.sum(matches.reshape(matches.shape[0], tok_count, TOPK).astype(jnp.float32), axis=2)


def build_tiles(token_rows, grad_rows, matches, flat_probs):
    select = select_matrix(matches, token_rows.shape[0]).astype(jnp.bfloat16)
    slot_scale = jnp.sum(jnp.where(matches, flat_probs[None, :], 0.0), axis=1)
    x_rows = jnp.dot(select, token_rows, preferred_element_type=jnp.float32).astype(jnp.bfloat16)
    g_rows = (
        jnp.dot(select, grad_rows, preferred_element_type=jnp.float32) * slot_scale[:, None]
    ).astype(jnp.bfloat16)
    return jnp.stack([x_rows, g_rows])


def expert_grads(tiles, w_gate, w_up, w_down):
    x_rows = tiles[:, 0]
    g_rows = tiles[:, 1]
    gate_pre = jnp.einsum("nsecd,edh->nsech", x_rows, w_gate, preferred_element_type=jnp.float32)
    up_pre = jnp.einsum("nsecd,edh->nsech", x_rows, w_up, preferred_element_type=jnp.float32)
    hidden_grad = jnp.einsum("nsecd,ehd->nsech", g_rows, w_down, preferred_element_type=jnp.float32)
    sigmoid_a = jax.nn.sigmoid(gate_pre)
    gate_grad = (hidden_grad * up_pre * sigmoid_a * (1.0 + gate_pre * (1.0 - sigmoid_a))).astype(
        jnp.bfloat16
    )
    up_grad = (hidden_grad * gate_pre * sigmoid_a).astype(jnp.bfloat16)
    partial_value = jnp.einsum(
        "nsech,edh->nsecd", gate_grad, w_gate, preferred_element_type=jnp.float32
    )
    partial_value = partial_value + jnp.einsum(
        "nsech,edh->nsecd", up_grad, w_up, preferred_element_type=jnp.float32
    )
    return partial_value.astype(jnp.bfloat16)


def on_device(tokens, out_grad, route_ids, route_probs, w_gate, w_up, w_down):
    columns = lax.axis_size("expert")
    local_experts = w_gate.shape[0]
    experts = local_experts * columns
    tok_count, width = tokens.shape
    capacity = max(2, 2 * tok_count * TOPK // experts)
    slots = experts * capacity
    tile_shape = (2, columns, local_experts, capacity, width)
    own_matches = slot_matches(route_ids.reshape(-1), experts, capacity)
    tiles = build_tiles(tokens, out_grad, own_matches, route_probs.reshape(-1)).reshape(
        (1,) + tile_shape
    )
    received = lax.all_to_all(tiles, "expert", split_axis=2, concat_axis=2, tiled=True)
    partials = expert_grads(
        lax.all_gather(received, "dp", axis=0, tiled=True), w_gate, w_up, w_down
    )
    summed = lax.psum_scatter(
        partials.astype(jnp.float32).astype(jnp.bfloat16), "dp", scatter_dimension=0, tiled=True
    ).astype(jnp.float32)
    returned = lax.all_to_all(
        summed.astype(jnp.bfloat16), "expert", split_axis=1, concat_axis=1, tiled=True
    ).astype(summed.dtype)
    own_select = select_matrix(own_matches, tok_count)
    result = jnp.dot(own_select.T, returned.reshape(slots, width), precision=lax.Precision.HIGHEST)
    return result.astype(jnp.bfloat16)


def solution(mesh):
    placed = (
        P(("dp", "expert"), None),
        P(("dp", "expert"), None),
        P(("dp", "expert"), None),
        P(("dp", "expert"), None),
        P("expert", None, "dp"),
        P("expert", None, "dp"),
        P("expert", "dp", None),
    )
    whole_block = dict(mesh.shape) == {"dp": 4, "expert": 8}

    def chosen(tokens, out_grad, route_ids, route_probs, w_gate, w_up, w_down):
        experts = w_gate.shape[0] * mesh.shape["expert"]
        dense = 2 * tokens.shape[0] * TOPK // experts >= tokens.shape[0]
        fits = tokens.shape[0] == 16 and experts <= LANES
        step = fused if whole_block and dense and fits else on_device
        return step(tokens, out_grad, route_ids, route_probs, w_gate, w_up, w_down)

    return jax.shard_map(
        chosen, mesh=mesh, in_specs=placed, out_specs=P(("dp", "expert"), None), check_vma=False
    )
```
